128 devices in a mesh: lon: 32 (over z_lo, y, x), lat: 4 (over z_hi, core).
Axes of the slice: x: 4, y: 4, z: 4 (z_hi: 2, z_lo: 2; z = z_hi * 2 + z_lo), core: 2. Of those that a mesh axis runs over, the one named last changes fastest.
Arguments:
- fields: bfloat16 [256, 128, 512], P('lon', 'lat'), may hold values from -6 to 6
- cotangent: bfloat16 [256, 128, 512], P('lon', 'lat'), may hold values from -16 to 16
- surface: int32 [256, 128], replicated, may hold values from 0 to 2
- qkv_weight: bfloat16 [2, 512, 1536], replicated, may hold values from -0.25 to 0.25
- proj_weight: bfloat16 [2, 512, 512], replicated, may hold values from -2 to 2
- norm_gain: float32 [2, 512], replicated, may hold values from 0.25 to 1.75
- log_scale: float32 [2, 16], replicated, may hold values from 1.4 to 3.4
- pos_table: float32 [2, 16, 64, 64], replicated, may hold values from -4 to 4
Outputs:
- d_fields: bfloat16 [256, 128, 512], P('lon', 'lat')
- d_qkv_weight: float32 [2, 512, 1536], P(None, ('lon', 'lat'))
- d_proj_weight: float32 [2, 512, 512], P(None, ('lon', 'lat'))
- d_norm_gain: float32 [2, 512], replicated
- d_log_scale: float32 [2, 16], replicated
- d_pos_table: float32 [2, 16, 64, 64], replicated
The draws below stay inside these ranges and needn't reach their ends.
All inputs are finite; a program needn't handle non-finite values.
Results may differ from the reference program's by a relative error of at most 0.03.
The reference program's roundings to bfloat16 on the way count: a program that leaves them out, or rounds other values in their place, can miss the bound.
Values may be sent and summed in bfloat16 or wider, within the bound.
A program may use at most 128 MiB of HBM per device.

```python
import math
import jax
import jax.numpy as jnp
from jax import lax

WIDTH = 512
HEADS = 16
WIN = 8
BLOCKS = 2
LON_CELLS = 256
LAT_CELLS = 128


def draw_cotangent(key, part):
    key = jax.random.fold_in(key, 11)
    lon_ramp = 1.0 + 2.0 * jnp.arange(LON_CELLS, dtype=jnp.float32) / max(LON_CELLS - 1, 1)
    noise = jnp.clip(jax.random.normal(key, (LON_CELLS, LAT_CELLS, WIDTH), jnp.float32), -6.0, 6.0)
    values = noise * lon_ramp[:, None, None] * 0.6
    return values.astype(jnp.bfloat16)


def draw_proj_weight(key, part):
    key = jax.random.fold_in(key, 23)
    first_key, second_key = jax.random.split(key)
    column = jnp.exp(jax.random.uniform(second_key, (BLOCKS, 1, WIDTH), jnp.float32, math.log(0.3), math.log(3.0)))
    base = jnp.clip(jax.random.normal(first_key, (BLOCKS, WIDTH, WIDTH), jnp.float32), -4.0, 4.0)
    return (base * column / math.sqrt(WIDTH)).astype(jnp.bfloat16)


def set_ends(values, own_key, smallest, top_value):
    longest = values.shape.index(max(values.shape))
    spots = []
    for shift in (0, 1):
        where = [jax.random.randint(jax.random.fold_in(own_key, axis), (), 0, length) for axis, length in enumerate(values.shape)]
        where[longest] = (where[longest] + shift) % values.shape[longest]
        spots.append(tuple(where))
    return values.at[spots[0]].set(smallest).at[spots[1]].set(top_value)


def level_of(rng, shape, cuts, smallest, high):
    def one(position, parts):
        steps = jax.random.uniform(jax.random.fold_in(jax.random.fold_in(rng, 6), position), (parts,), jnp.float32, smallest / len(cuts), high / len(cuts))
        return jnp.repeat(jnp.exp(steps), shape[position] // parts).reshape((-1,) + (1,) * (len(shape) - position - 1))

    level = one(*cuts[0])
    for cut in cuts[1:]:
        level = level * one(*cut)
    return level


def scatter_about(stream_key, extent, scale, most, cuts=(), kind=jnp.bfloat16):
    drawn = scale * jax.random.normal(stream_key, extent, jnp.float32)
    if cuts:
        drawn = drawn * level_of(stream_key, extent, cuts, -0.22, 0.18)
    return jnp.clip(drawn, -most, most).astype(kind)


def setup_inputs(seed: int = 0) -> dict:
    seeds = jax.random.split(jax.random.key(seed), 9)
    fields = scatter_about(seeds[0], (LON_CELLS, LAT_CELLS, WIDTH), 1.0, 6.0, ((0, 32), (1, 4)))
    cotangent = draw_cotangent(jax.random.fold_in(seeds[8], 71), 0)
    surface = set_ends(jax.random.randint(seeds[2], (LON_CELLS, LAT_CELLS), 0, 3), jax.random.fold_in(seeds[2], 1), 0, 2).astype(jnp.int32)
    qkv_weight = scatter_about(seeds[3], (BLOCKS, WIDTH, 3 * WIDTH), WIDTH ** -0.5, 0.25)
    proj_weight = draw_proj_weight(jax.random.fold_in(seeds[8], 71), 0)
    norm_gain = jnp.clip(1.0 + 0.15 * jax.random.normal(seeds[5], (BLOCKS, WIDTH), jnp.float32), 0.25, 1.75)
    log_scale = jnp.clip(jax.random.uniform(seeds[6], (BLOCKS, HEADS), jnp.float32, 1.4, 3.4), 1.4, 3.4)
    pos_table = scatter_about(seeds[7], (BLOCKS, HEADS, WIN * WIN, WIN * WIN), 1.0, 4.0, (), jnp.float32)
    return dict(fields=fields, cotangent=cotangent, surface=surface, qkv_weight=qkv_weight, proj_weight=proj_weight, norm_gain=norm_gain, log_scale=log_scale, pos_table=pos_table)


NORM_EPS = 1e-06
LAYER_EPS = 1e-05
BIAS_CAP = 16.0

def window_grid(grid):
    rest = grid.shape[2:]
    lon_total = grid.shape[0]
    lat_total = grid.shape[1]
    blocks = grid.reshape((lon_total // WIN, WIN, lat_total // WIN, WIN) + rest)
    blocks = jnp.swapaxes(blocks, 1, 2)
    return blocks.reshape((lon_total // WIN, lat_total // WIN, WIN * WIN) + rest)

def grid_back(blocks):
    rest = blocks.shape[3:]
    outer = blocks.shape[0]
    inner = blocks.shape[1]
    grid = blocks.reshape((outer, inner, WIN, WIN) + rest)
    grid = jnp.swapaxes(grid, 1, 2)
    return grid.reshape((outer * WIN, inner * WIN) + rest)

def pair_mask(labels):
    return labels[..., :, None] == labels[..., None, :]

def widen(half):
    return lax.optimization_barrier(half).astype(jnp.float32)

def attend_forward(tokens, allowed, w_inner, w_outer, gain, log_gain, table):
    count, length, width = tokens.shape
    heads = log_gain.shape[0]
    depth = width // heads
    flat = tokens.reshape(count * length, width)
    mixed = jnp.dot(flat, w_inner, preferred_element_type=jnp.float32)
    mixed = mixed.reshape(count, length, 3, heads, depth)
    query = mixed[:, :, 0]
    keys = mixed[:, :, 1]
    values = mixed[:, :, 2].astype(jnp.bfloat16)
    query_len = jnp.sqrt(lax.optimization_barrier(jnp.sum(query * query, axis=-1, keepdims=True)) + NORM_EPS)
    key_len = jnp.sqrt(lax.optimization_barrier(jnp.sum(keys * keys, axis=-1, keepdims=True)) + NORM_EPS)
    query_unit = query / query_len
    key_unit = keys / key_len
    query_half = query_unit.astype(jnp.bfloat16)
    key_half = key_unit.astype(jnp.bfloat16)
    cosine = jnp.einsum('wihd,wjhd->whij', widen(query_half), widen(key_half))
    scale = jnp.exp(log_gain)[:, None, None]
    scores = cosine * scale + BIAS_CAP * jax.nn.sigmoid(table)
    expo = jnp.where(allowed[:, None], jnp.exp(scores - scale - BIAS_CAP), jnp.float32(0.0))
    probs = expo / lax.optimization_barrier(jnp.sum(expo, axis=-1, keepdims=True))
    probs_half = probs.astype(jnp.bfloat16)
    attended = jnp.einsum('whij,wjhd->wihd', widen(probs_half), widen(values))
    attended = attended.astype(jnp.bfloat16).reshape(count * length, width)
    projected = jnp.dot(attended, w_outer, preferred_element_type=jnp.float32)
    centred = projected - lax.optimization_barrier(jnp.mean(projected, axis=-1, keepdims=True))
    inverse = lax.rsqrt(lax.optimization_barrier(jnp.mean(centred * centred, axis=-1, keepdims=True)) + LAYER_EPS)
    normed = centred * inverse
    output = (flat.astype(jnp.float32) + normed * gain).astype(jnp.bfloat16)
    saved = (flat, query_unit, key_unit, query_len, key_len, query_half, key_half, values, cosine, probs, probs_half, attended, normed, inverse)
    return (output.reshape(count, length, width), saved)

def attend_backward(upstream, saved, w_inner, w_outer, gain, log_gain, table):
    flat, query_unit, key_unit, query_len, key_len, query_half, key_half, values, cosine, probs, probs_half, attended, normed, inverse = saved
    count = probs.shape[0]
    heads = probs.shape[1]
    width = flat.shape[1]
    depth = width // heads
    grad_out = upstream.reshape(flat.shape[0], width).astype(jnp.float32)
    gain_term = lax.optimization_barrier(jnp.sum(grad_out * normed, axis=0))
    scaled = grad_out * gain
    grad_proj = inverse * (scaled - lax.optimization_barrier(jnp.mean(scaled, axis=-1, keepdims=True)) - normed * lax.optimization_barrier(jnp.mean(scaled * normed, axis=-1, keepdims=True)))
    grad_proj = grad_proj.astype(jnp.bfloat16)
    grad_att = jnp.dot(grad_proj, w_outer.T, preferred_element_type=jnp.float32)
    grad_att = grad_att.astype(jnp.bfloat16).reshape(count, -1, heads, depth)
    grad_values = jnp.einsum('whij,wihd->wjhd', widen(probs_half), widen(grad_att))
    grad_probs = jnp.einsum('wihd,wjhd->whij', widen(grad_att), widen(values))
    grad_scores = probs * (grad_probs - lax.optimization_barrier(jnp.sum(probs * grad_probs, axis=-1, keepdims=True)))
    scale = jnp.exp(log_gain)
    sigma = jax.nn.sigmoid(table)
    table_term = lax.optimization_barrier(jnp.sum(grad_scores, axis=0)) * (BIAS_CAP * sigma * (1.0 - sigma))
    log_term = scale * lax.optimization_barrier(jnp.sum(grad_scores * cosine, axis=(0, 2, 3)))
    grad_cos = (grad_scores * scale[:, None, None]).astype(jnp.bfloat16)
    grad_qunit = jnp.einsum('whij,wjhd->wihd', widen(grad_cos), widen(key_half))
    grad_kunit = jnp.einsum('whij,wihd->wjhd', widen(grad_cos), widen(query_half))
    grad_query = (grad_qunit - query_unit * lax.optimization_barrier(jnp.sum(query_unit * grad_qunit, axis=-1, keepdims=True))) / query_len
    grad_keys = (grad_kunit - key_unit * lax.optimization_barrier(jnp.sum(key_unit * grad_kunit, axis=-1, keepdims=True))) / key_len
    grad_mixed = jnp.stack([grad_query, grad_keys, grad_values], axis=2)
    grad_mixed = grad_mixed.astype(jnp.bfloat16).reshape(-1, 3 * width)
    grad_tokens = grad_out + jnp.dot(grad_mixed, w_inner.T, preferred_element_type=jnp.float32)
    grad_tokens = grad_tokens.astype(jnp.bfloat16).reshape(count, -1, width)
    return (grad_tokens, grad_mixed, grad_proj, (gain_term, log_term, table_term))

def run_forward(token_grid, allow_grid, params):

    def one_row(item):
        return attend_forward(item[0], item[1], *params)[0]
    return lax.map(one_row, (token_grid, allow_grid))

def run_backward(token_grid, upstream_grid, allow_grid, params):
    width = params[0].shape[0]
    heads = params[3].shape[0]
    start = (jnp.zeros((width, 3 * width), jnp.float32), jnp.zeros((width, width), jnp.float32), jnp.zeros((width,), jnp.float32), jnp.zeros((heads,), jnp.float32), jnp.zeros(params[4].shape, jnp.float32))

    def one_row(carry, item):
        tokens, upstream, allowed = item
        _, saved = attend_forward(tokens, allowed, *params)
        grad_tokens, grad_mixed, grad_proj, small = attend_backward(upstream, saved, *params)
        inner_term = jnp.dot(saved[0].T, grad_mixed, preferred_element_type=jnp.float32)
        outer_term = jnp.dot(saved[11].T, grad_proj, preferred_element_type=jnp.float32)
        summed = (carry[0] + inner_term, carry[1] + outer_term, carry[2] + small[0], carry[3] + small[1], carry[4] + small[2])
        return (summed, grad_tokens)
    return lax.scan(one_row, start, (token_grid, upstream_grid, allow_grid))

def reference(fields, cotangent, surface, qkv_weight, proj_weight, norm_gain, log_scale, pos_table):
    margin = WIN // 2
    lon_total, lat_total, width = fields.shape
    factor = 1.0 / math.sqrt(lon_total * lat_total)
    first = (qkv_weight[0], proj_weight[0], norm_gain[0], log_scale[0], pos_table[0])
    second = (qkv_weight[1], proj_weight[1], norm_gain[1], log_scale[1], pos_table[1])
    allow_first = pair_mask(window_grid(surface))
    north_rim = ((jnp.arange(lat_total, dtype=jnp.int32) + margin) % lat_total < margin).astype(jnp.int32)
    rolled_key = jnp.roll(surface, (-margin, -margin), (0, 1)) * 2 + north_rim[None, :]
    allow_second = pair_mask(window_grid(rolled_key))
    field_grid = window_grid(fields)
    hidden = grid_back(run_forward(field_grid, allow_first, first))
    rolled_hidden = jnp.roll(hidden, (-margin, -margin), (0, 1))
    rolled_grad = jnp.roll(cotangent, (-margin, -margin), (0, 1))
    sums_second, grad_rolled = run_backward(window_grid(rolled_hidden), window_grid(rolled_grad), allow_second, second)
    grad_hidden = jnp.roll(grid_back(grad_rolled), (margin, margin), (0, 1))
    sums_first, grad_fields = run_backward(field_grid, window_grid(grad_hidden), allow_first, first)
    d_fields = grid_back(grad_fields)
    d_qkv = jnp.stack([sums_first[0], sums_second[0]]) * factor
    d_proj = jnp.stack([sums_first[1], sums_second[1]]) * factor
    d_gain = jnp.stack([sums_first[2], sums_second[2]]) * factor
    d_log = jnp.stack([sums_first[3], sums_second[3]]) * factor
    d_table = jnp.stack([sums_first[4], sums_second[4]]) * factor
    return (d_fields, d_qkv, d_proj, d_gain, d_log, d_table)
```

```python
import math

import jax
import jax.numpy as jnp
import numpy as np
from jax import lax
from jax.experimental import pallas as pl
from jax.experimental.pallas import tpu as pltpu
from jax.sharding import PartitionSpec as P

WIN = 8
HALF = WIN // 2
LON, LAT = 8, 32
TOKENS = LON * LAT
WINDOWS = 4
WIDTH = 512
GROUPS = 4
PART = 768
NORM_EPS = 1e-06
LAYER_EPS = 1e-05
CAP = 16.0
F32, BF16 = jnp.float32, jnp.bfloat16
MESH = pl.DeviceIdType.MESH

ORDERS = (("x", "y", "z"), ("y", "z", "x"), ("z", "x", "y"))


def token_orders():
    cells = [(i, l) for i in range(LON) for l in range(LAT)]
    natural = {c: k for k, c in enumerate(cells)}
    windows = [(i, w * WIN + j) for w in range(WINDOWS) for i in range(WIN) for j in range(WIN)]
    spot = {c: k for k, c in enumerate(windows)}
    parts = []
    for north in (False, True):
        for west in (False, True):
            parts += [c for c in cells if (c[0] < HALF) == west and (c[1] < HALF) == north]
    to_window = np.zeros((TOKENS, TOKENS), np.float32)
    to_part = np.zeros_like(to_window)
    window_to_part = np.zeros_like(to_window)
    to_shifted = np.zeros_like(to_window)
    for k, c in enumerate(windows):
        to_window[k, natural[c]] = 1
    for k, c in enumerate(parts):
        to_part[k, natural[c]] = 1
        window_to_part[k, spot[c]] = 1
        to_shifted[spot[((c[0] - HALF) % LON, (c[1] - HALF) % LAT)], k] = 1
    picks = [to_window, window_to_part, to_part, to_shifted]
    picks += [to_window.T, window_to_part.T, to_shifted.T]
    return np.stack(picks)


def row_orders():
    orders = np.zeros((3, WIDTH, WIDTH), np.float32)
    for g, axes in enumerate(ORDERS):
        for place in range(WIDTH):
            at = dict(core=place // 256)
            for axis, step in zip(axes, (64, 16, 4)):
                at[axis] = place // step % 4
            lon = at["z"] % 2 * 16 + at["y"] * 4 + at["x"]
            lat = at["z"] // 2 * 2 + at["core"]
            orders[g, place, (lon * 4 + lat) * 4 + place % 4] = 1
    return orders


def mm(a, b):
    return jnp.dot(a, b, preferred_element_type=F32)


def mm_nt(a, b):
    return lax.dot_general(a, b, (((1,), (1,)), ((), ())), preferred_element_type=F32)


def mm_tn(a, b):
    return lax.dot_general(a, b, (((0,), (0,)), ((), ())), preferred_element_type=F32)


def iota(shape, dim):
    return lax.broadcasted_iota(jnp.int32, shape, dim)


def same_run(size, run):
    return (iota((size, size), 0) // run == iota((size, size), 1) // run).astype(F32).astype(BF16)


def run_sum(x, ones):
    high = x.astype(BF16)
    low = (x - high.astype(F32)).astype(BF16)
    return mm(high, ones) + mm(low, ones)


def scratch_spec():
    v = pltpu.VMEM
    return dict(
        x=v((2, TOKENS, WIDTH), BF16),
        grad=v((TOKENS, WIDTH), BF16),
        qunit=v((2, TOKENS, WIDTH), F32),
        kunit=v((2, TOKENS, WIDTH), F32),
        qinv=v((2, TOKENS, WIDTH), F32),
        kinv=v((2, TOKENS, WIDTH), F32),
        qhalf=v((2, TOKENS, WIDTH), BF16),
        khalf=v((2, TOKENS, WIDTH), BF16),
        vhalf=v((2, TOKENS, WIDTH), BF16),
        cosine=v((2, GROUPS, TOKENS, 256), F32),
        probs=v((2, GROUPS, TOKENS, 256), F32),
        attended=v((2, TOKENS, WIDTH), BF16),
        normed=v((2, TOKENS, WIDTH), F32),
        inverse=v((2, TOKENS, 1), F32),
        dz=v((TOKENS, WIDTH), BF16),
        datt=v((TOKENS, WIDTH), BF16),
        dmixed=v((TOKENS, 3 * WIDTH), BF16),
        bias=v((2, GROUPS, 64, 256), F32),
        slope=v((2, GROUPS, 64, 256), F32),
        scale=v((2, GROUPS, 1, 256), F32),
        mask=v((2, TOKENS, 256), F32),
        dtab=v((GROUPS, 64, 256), F32),
        dlog=v((GROUPS, 1, 256), F32),
        hid_out=v((TOKENS, WIDTH), BF16),
        hid_in=v((TOKENS, WIDTH), BF16),
        cot_out=v((TOKENS, WIDTH), BF16),
        cot_in=v((TOKENS, WIDTH), BF16),
        back_out=v((TOKENS, WIDTH), BF16),
        back_in=v((TOKENS, WIDTH), BF16),
        part=v((2, 3, WIDTH, PART), BF16),
        r1=v((2, 3, 256, PART), BF16),
        s1=v((2, 3, 256, PART), BF16),
        r2=v((2, 3, 3, 64, PART), BF16),
        s2=v((2, 3, 64, PART), BF16),
        r3=v((2, 3, 3, 16, PART), BF16),
        r4=v((2, 3, 4, 16, PART), BF16),
        small=v((2, WIDTH, 256), BF16),
        send=pltpu.SemaphoreType.DMA((96,)),
        recv=pltpu.SemaphoreType.DMA((96,)),
    )


class Refs:
    pass


class Links:
    def __init__(self, r):
        self.r = r
        self.count = 0
        self.started = []
        lon, lat = lax.axis_index("lon"), lax.axis_index("lat")
        self.lon, self.lat = lon, lat
        self.core = lat % 2
        self.at = dict(x=lon % 4, y=lon // 4 % 4, z=lat // 2 * 2 + lon // 16)

    def along(self, axis, to):
        at = dict(self.at)
        at[axis] = to
        return (at["z"] % 2 * 16 + at["y"] * 4 + at["x"], at["z"] // 2 * 2 + self.core)

    def sibling(self):
        return (self.lon, self.lat // 2 * 2 + 1 - self.core)

    def shifted(self, dlon, dlat):
        return ((self.lon + dlon + 32) % 32, (self.lat + dlat + 4) % 4)

    def meet(self):
        barrier = pltpu.get_barrier_semaphore()
        others = [self.sibling()]
        for axis in ("x", "y", "z"):
            others += [self.along(axis, (self.at[axis] + d) % 4) for d in (1, 2, 3)]
        for d in (-1, 1):
            others += [self.shifted(d, 0), self.shifted(0, d), self.shifted(d, d)]
        for other in others:
            pl.semaphore_signal(barrier, inc=1, device_id=other, device_id_type=MESH)
        pl.semaphore_wait(barrier, len(others))

    def send(self, src, dst, to):
        k = self.count
        self.count += 1
        copy = pltpu.make_async_remote_copy(
            src_ref=src, dst_ref=dst, send_sem=self.r.send.at[k], recv_sem=self.r.recv.at[k],
            device_id=to, device_id_type=MESH,
        )
        copy.start()
        self.started.append(copy)
        return copy

    def finish(self):
        for copy in self.started:
            copy.wait_send()

    def halo(self, src, dst, sign):
        dst[0:112, :] = src[0:112, :]
        spans = ((112, 112, (sign, 0)), (224, 16, (0, sign)), (240, 16, (sign, sign)))
        return [
            self.send(src.at[pl.ds(o, n)], dst.at[pl.ds(o, n)], self.shifted(*to))
            for o, n, to in spans
        ]


class Reduce:
    def __init__(self, r, links, b, g):
        self.r, self.links, self.b, self.g = r, links, b, g
        self.axes = ORDERS[g]
        self.place = [links.at[a] for a in self.axes]
        self.step = 0

    def peers(self, level):
        axis, place = self.axes[level], self.place[level]
        return [((place + d) % 4, d) for d in (1, 2, 3)]

    def rows(self, at, size):
        return pl.ds(pl.multiple_of(at * size, size), size)

    def advance(self):
        r, links, b, g = self.r, self.links, self.b, self.g
        step = self.step
        self.step += 1
        if step == 0:
            src = r.part.at[b, g, self.rows(1 - links.core, 256)]
            self.waits = [links.send(src, r.r1.at[b, g], links.sibling())]
            return
        for copy in self.waits:
            copy.wait_recv()
        if step == 1:
            own = r.part[b, g, self.rows(links.core, 256), :].astype(F32)
            r.s1[b, g] = (own + r.r1[b, g].astype(F32)).astype(BF16)
            self.waits = [
                links.send(r.s1.at[b, g, self.rows(k, 64)], r.r2.at[b, g, d - 1], links.along(self.axes[0], k))
                for k, d in self.peers(0)
            ]
        elif step == 2:
            total = r.s1[b, g, self.rows(self.place[0], 64), :].astype(F32)
            for d in range(3):
                total += r.r2[b, g, d].astype(F32)
            r.s2[b, g] = total.astype(BF16)
            self.waits = [
                links.send(r.s2.at[b, g, self.rows(k, 16)], r.r3.at[b, g, d - 1], links.along(self.axes[1], k))
                for k, d in self.peers(1)
            ]
        elif step == 3:
            total = r.s2[b, g, self.rows(self.place[1], 16), :].astype(F32)
            for d in range(3):
                total += r.r3[b, g, d].astype(F32)
            mine = r.r4.at[b, g, self.place[2]]
            mine[...] = total.astype(BF16)
            self.waits = [links.send(mine, mine, links.along(self.axes[2], k)) for k, d in self.peers(2)]
        elif step == 4:
            total = r.r4[b, g, 0].astype(F32)
            for k in range(1, 4):
                total += r.r4[b, g, k].astype(F32)
            own = total[0:4, :]
            for k in range(1, 4):
                own = jnp.where(self.place[2] == k, total[4 * k : 4 * k + 4, :], own)
            if g == 0:
                r.d_proj[b] = own[:, 0:WIDTH]
                at = links.core * 16 + self.place[0] * 4 + self.place[1]
                mine = r.small.at[b, self.rows(at, 16)]
                mine[...] = total[:, WIDTH:PART].astype(BF16)
                self.waits = [links.send(mine, mine, links.along(self.axes[1], k)) for k, d in self.peers(1)]
            else:
                r.d_qkv[b, :, (g - 1) * PART : g * PART] = own
        elif step == 5:
            mine = r.small.at[b, self.rows(links.core * 4 + self.place[0], 64)]
            self.waits = [links.send(mine, mine, links.along(self.axes[0], k)) for k, d in self.peers(0)]
        elif step == 6:
            mine = r.small.at[b, self.rows(links.core, 256)]
            self.waits = [links.send(mine, mine, links.sibling())]
        elif step == 7:
            for h in range(16):
                piece = r.small[b, (h // 2) * 64 : (h // 2) * 64 + 64, 0:128].astype(F32)
                r.d_table[b, h] = piece[:, h % 2 * 64 : h % 2 * 64 + 64]
            rest = r.small[b, 0:16, 128:256].astype(F32)
            for k in range(4):
                r.d_gain[b : b + 1, k * 128 : k * 128 + 128] = rest[k : k + 1, :]
            lane = iota((1, 16), 1)
            row = jnp.zeros((1, 16), F32)
            for h in range(16):
                spot = rest[8 + h // 2 : 9 + h // 2, h % 2 * 64 : h % 2 * 64 + 1]
                row = jnp.where(lane == h, spot, row)
            r.d_log[b : b + 1, :] = row


def tables(r, b):
    lane = iota((1, 256), 1) // 64
    for g in range(GROUPS):
        logs = jnp.full((1, 256), 0.0, F32) + r.log_scale[b, 4 * g]
        for h in range(1, 4):
            logs = jnp.where(lane == h, r.log_scale[b, 4 * g + h], logs)
        scale = jnp.exp(logs)
        sigma = jnp.concatenate([r.pos_table[b, 4 * g + h] for h in range(4)], axis=1)
        sigma = 1.0 / (1.0 + jnp.exp(-sigma))
        r.scale[b, g] = scale
        r.bias[b, g] = CAP * sigma - scale - CAP
        r.slope[b, g] = CAP * sigma * (1.0 - sigma)


def masks(r, links, b):
    shift = HALF * b
    first = r.surface[pl.ds(pl.multiple_of(links.lon * LON, LON), LON), :]
    later = r.surface[pl.ds(pl.multiple_of((links.lon + 1) % 32 * LON, LON), LON), :]
    slab = jnp.concatenate([first, later], axis=0).astype(F32).astype(BF16)

    def column(w, t):
        return (links.lat * LAT + w * WIN + t % WIN + shift) % 128

    def labels(found, col):
        return found * 2.0 + (col < shift).astype(F32)

    for w in range(WINDOWS):
        tok = iota((128, 256), 1) % 64
        pick = (iota((128, 256), 0) == column(w, tok)).astype(F32).astype(BF16)
        wide = mm(slab, pick)
        tok = iota((16, 256), 1) % 64
        found = jnp.sum(jnp.where(iota((16, 256), 0) == tok // WIN + shift, wide, 0.0), axis=0, keepdims=True)
        along = labels(found, column(w, iota((1, 256), 1) % 64))
        tok = iota((64, 128), 0)
        pick = (iota((64, 128), 1) == column(w, tok)).astype(F32).astype(BF16)
        tall = mm_nt(pick, slab)
        tok = iota((64, 16), 0)
        found = jnp.sum(jnp.where(iota((64, 16), 1) == tok // WIN + shift, tall, 0.0), axis=1, keepdims=True)
        down = labels(found, column(w, iota((64, 1), 0)))
        r.mask[b, w * 64 : w * 64 + 64, :] = (down == along).astype(F32)


def group_lanes(g, base=0):
    return pl.ds(pl.multiple_of(base + g * 128, 128), 128)


def head_lanes(dtype):
    lane = iota((1, 128), 1) // 32
    return [(lane == h).astype(F32).astype(dtype) for h in range(4)]


def expand(block, lanes):
    return jnp.concatenate([block * lanes[h] for h in range(4)], axis=0)


def collapse(block, lanes):
    return sum(block[h * 64 : h * 64 + 64, :] * lanes[h] for h in range(4))


def window(x, w):
    return x[w * 64 : w * 64 + 64, :]


def forward(r, b, last):
    x = r.x[b]
    ones32 = same_run(256, 32)
    for name, k in (("q", 0), ("k", 1)):
        mixed = mm(x, r.qkv_weight[b, :, k * WIDTH : (k + 1) * WIDTH])
        square = mixed * mixed
        total = jnp.concatenate([run_sum(square[:, o : o + 256], ones32) for o in (0, 256)], axis=1)
        inv = lax.rsqrt(total + NORM_EPS)
        unit = mixed * inv
        getattr(r, name + "inv")[b] = inv
        getattr(r, name + "unit")[b] = unit
        getattr(r, name + "half")[b] = unit.astype(BF16)
    r.vhalf[b] = mm(x, r.qkv_weight[b, :, 2 * WIDTH : 3 * WIDTH]).astype(BF16)

    def attend(g, carry):
        cols = group_lanes(g)
        lanes = head_lanes(BF16)
        ones64 = same_run(256, 64)
        q, k, v = r.qhalf[b, :, cols], r.khalf[b, :, cols], r.vhalf[b, :, cols]
        cosine = jnp.concatenate(
            [mm_nt(window(q, w), expand(window(k, w), lanes)) for w in range(WINDOWS)], axis=0
        )
        r.cosine[b, g] = cosine
        bias = jnp.concatenate([r.bias[b, g]] * WINDOWS, axis=0)
        expo = jnp.exp(cosine * r.scale[b, g] + bias) * r.mask[b]
        probs = expo / run_sum(expo, ones64)
        r.probs[b, g] = probs
        half = probs.astype(BF16)
        out = [mm(window(half, w), expand(window(v, w), lanes)) for w in range(WINDOWS)]
        r.attended[b, :, cols] = jnp.concatenate(out, axis=0).astype(BF16)
        return carry

    lax.fori_loop(0, GROUPS, attend, 0)
    z = mm(r.attended[b], r.proj_weight[b])
    centred = z - jnp.mean(z, axis=-1, keepdims=True)
    inverse = lax.rsqrt(jnp.mean(centred * centred, axis=-1, keepdims=True) + LAYER_EPS)
    normed = centred * inverse
    r.inverse[b] = inverse
    r.normed[b] = normed
    if last:
        return None
    return (x.astype(F32) + normed * r.norm_gain[b : b + 1, :]).astype(BF16)


def backward_norm(r, b, factor):
    grad = r.grad[...].astype(F32)
    normed = r.normed[b]
    gain_term = jnp.sum(grad * normed, axis=0, keepdims=True) * factor
    for k in range(4):
        r.part[b, 0, 0:16, 640:768] = jnp.where(
            iota((16, 128), 0) == k, gain_term[:, k * 128 : k * 128 + 128], r.part[b, 0, 0:16, 640:768].astype(F32)
        ).astype(BF16)
    scaled = grad * r.norm_gain[b : b + 1, :]
    first = jnp.mean(scaled, axis=-1, keepdims=True)
    second = jnp.mean(scaled * normed, axis=-1, keepdims=True)
    dz = (r.inverse[b] * (scaled - first - normed * second)).astype(BF16)
    r.dz[...] = dz
    r.datt[...] = mm_nt(dz, r.proj_weight[b]).astype(BF16)


def backward_attend(r, b, begin, end):
    def attend(g, carry):
        cols = group_lanes(g)
        lanes, wide = head_lanes(BF16), head_lanes(F32)
        ones64, ones32 = same_run(256, 64), same_run(128, 32)
        q, k, v = r.qhalf[b, :, cols], r.khalf[b, :, cols], r.vhalf[b, :, cols]
        datt = r.datt[:, cols]
        probs = r.probs[b, g]
        half = probs.astype(BF16)
        dprobs = jnp.concatenate(
            [mm_nt(window(datt, w), expand(window(v, w), lanes)) for w in range(WINDOWS)], axis=0
        )
        dscores = probs * (dprobs - run_sum(probs * dprobs, ones64))
        r.dtab[g] = sum(window(dscores, w) for w in range(WINDOWS))
        r.dlog[g] = jnp.sum(dscores * r.cosine[b, g], axis=0, keepdims=True)
        dcos = (dscores * r.scale[b, g]).astype(BF16)
        dq, dk, dv = [], [], []
        for w in range(WINDOWS):
            dq.append(mm(window(dcos, w), expand(window(k, w), lanes)))
            dk.append(collapse(mm_tn(window(dcos, w), window(q, w)), wide))
            dv.append(collapse(mm_tn(window(half, w), window(datt, w)), wide))
        for base, parts, unit, inv in ((0, dq, r.qunit, r.qinv), (WIDTH, dk, r.kunit, r.kinv)):
            grad = jnp.concatenate(parts, axis=0)
            unit = unit[b, :, cols]
            grad = (grad - unit * run_sum(unit * grad, ones32)) * inv[b, :, cols]
            r.dmixed[:, group_lanes(g, base)] = grad.astype(BF16)
        r.dmixed[:, group_lanes(g, 2 * WIDTH)] = jnp.concatenate(dv, axis=0).astype(BF16)
        return carry

    lax.fori_loop(begin, end, attend, 0)


def backward_tokens(r, b):
    grad = r.grad[...].astype(F32) + mm_nt(r.dmixed[...], r.qkv_weight[b])
    return grad.astype(BF16)


def small_part(r, b, factor):
    ones64 = same_run(256, 64)
    sums = []
    for g in range(GROUPS):
        term = (r.dtab[g] * r.slope[b, g] * factor).astype(BF16)
        r.part[b, 0, g * 128 : g * 128 + 64, 512:640] = term[:, 0:128]
        r.part[b, 0, g * 128 + 64 : g * 128 + 128, 512:640] = term[:, 128:256]
        sums.append(run_sum(jnp.concatenate([r.dlog[g]] * 8, axis=0), ones64) * (r.scale[b, g] * factor))
    row = iota((16, 128), 0)
    rest = r.part[b, 0, 0:16, 640:768].astype(F32)
    for g in range(GROUPS):
        for k in range(2):
            rest = jnp.where(row == 8 + 2 * g + k, sums[g][0:1, k * 128 : k * 128 + 128], rest)
    r.part[b, 0, 0:16, 640:768] = rest.astype(BF16)


def weight_part(r, b, g, factor):
    if g == 0:
        turned = mm_nt(r.row_order[0], r.attended[b]).astype(BF16)
        r.part[b, 0, :, 0:WIDTH] = (mm(turned, r.dz[...]) * factor).astype(BF16)
    else:
        turned = mm_nt(r.row_order[g], r.x[b]).astype(BF16)
        grad = mm(turned, r.dmixed[:, (g - 1) * PART : g * PART])
        r.part[b, g] = (grad * factor).astype(BF16)


INPUTS = (
    "fields", "cotangent", "surface", "qkv_weight", "proj_weight", "norm_gain", "log_scale", "pos_table",
    "token_order", "row_order",
)
OUTPUTS = ("d_fields", "d_qkv", "d_proj", "d_gain", "d_log", "d_table")


def pick(order, block):
    return mm(order, block).astype(BF16)


def kernel(factor, *refs):
    r = Refs()
    for name, ref in zip(INPUTS + OUTPUTS + tuple(scratch_spec()), refs):
        setattr(r, name, ref)
    links = Links(r)
    links.meet()
    to_window, window_to_part, to_part, to_shifted, from_window, part_to_window, from_shifted = range(7)
    order = r.token_order

    r.cot_out[...] = pick(order[to_part], r.cotangent[...])
    cot = links.halo(r.cot_out, r.cot_in, -1)
    for b in range(2):
        tables(r, b)
        masks(r, links, b)
        r.part[b, 0, :, 640:768] = jnp.zeros((WIDTH, 128), BF16)
    r.x[0] = pick(order[to_window], r.fields[...])
    hidden = forward(r, 0, False)
    r.hid_out[...] = pick(order[window_to_part], hidden)
    hid = links.halo(r.hid_out, r.hid_in, -1)
    for copy in cot + hid:
        copy.wait_recv()
    r.x[1] = pick(order[to_shifted], r.hid_in[...])
    r.grad[...] = pick(order[to_shifted], r.cot_in[...])
    forward(r, 1, True)
    backward_norm(r, 1, factor)
    backward_attend(r, 1, 0, GROUPS)
    r.back_out[...] = pick(order[from_shifted], backward_tokens(r, 1))
    back = links.halo(r.back_out, r.back_in, 1)
    second = [Reduce(r, links, 1, g) for g in range(3)]
    first = [Reduce(r, links, 0, g) for g in range(3)]
    small_part(r, 1, factor)
    for g in range(3):
        weight_part(r, 1, g, factor)
        second[g].advance()
    for copy in back:
        copy.wait_recv()
    r.grad[...] = pick(order[part_to_window], r.back_in[...])
    backward_norm(r, 0, factor)
    for job in second:
        job.advance()
    for g in range(GROUPS):
        backward_attend(r, 0, g, g + 1)
        for job in second:
            if g < 3:
                job.advance()
    small_part(r, 0, factor)
    weight_part(r, 0, 0, factor)
    first[0].advance()
    second[0].advance()
    for g in (1, 2):
        weight_part(r, 0, g, factor)
        first[g].advance()
    second[0].advance()
    r.d_fields[...] = pick(order[from_window], backward_tokens(r, 0))
    second[0].advance()
    for step in range(4):
        for job in first:
            job.advance()
    for step in range(3):
        first[0].advance()
    links.finish()


def local(fields, cotangent, surface, qkv_weight, proj_weight, norm_gain, log_scale, pos_table):
    factor = 1.0 / math.sqrt(TOKENS * 128)
    shape = jax.ShapeDtypeStruct
    orders = [jnp.asarray(x, BF16) for x in (token_orders(), row_orders())]
    vmem = pl.BlockSpec(memory_space=pltpu.VMEM)
    smem = pl.BlockSpec(memory_space=pltpu.SMEM)

    def body(*refs):
        kernel(factor, *refs)

    out = pl.pallas_call(
        body,
        out_shape=[
            shape((TOKENS, WIDTH), BF16),
            shape((2, 4, 3 * WIDTH), F32),
            shape((2, 4, WIDTH), F32),
            shape((2, WIDTH), F32),
            shape((2, 16), F32),
            shape((2, 16, 64, 64), F32),
        ],
        in_specs=[vmem] * 6 + [smem] + [vmem] * 3,
        out_specs=[vmem] * 6,
        scratch_shapes=list(scratch_spec().values()),
        compiler_params=pltpu.CompilerParams(
            collective_id=0, has_side_effects=True, vmem_limit_bytes=60 * 1024 * 1024
        ),
    )(
        fields.reshape(TOKENS, WIDTH), cotangent.reshape(TOKENS, WIDTH), surface, qkv_weight, proj_weight,
        norm_gain, log_scale, pos_table, *orders,
    )
    return (out[0].reshape(LON, LAT, WIDTH),) + tuple(out[1:])


def solution(mesh):
    placed = (P("lon", "lat", None), P("lon", "lat", None), P(), P(), P(), P(), P(), P())
    return jax.shard_map(
        local,
        mesh=mesh,
        in_specs=placed,
        out_specs=(
            P("lon", "lat", None),
            P(None, ("lon", "lat"), None),
            P(None, ("lon", "lat"), None),
            P(),
            P(),
            P(),
        ),
        check_vma=False,
    )
```

```python
import math

import jax
import jax.numpy as jnp
import numpy as np
from jax import lax
from jax.experimental import pallas as pl
from jax.experimental.pallas import tpu as pltpu
from jax.sharding import PartitionSpec as P

WIN = 8
HALF = WIN // 2
LON, LAT = 8, 32
TOKENS = LON * LAT
WINDOWS = 4
WIDTH = 512
GROUPS = 4
PARTS = 4
HALFROWS = 288
PIECE = 96
NORM_EPS = 1e-06
LAYER_EPS = 1e-05
CAP = 16.0
F32, BF16 = jnp.float32, jnp.bfloat16
MESH = pl.DeviceIdType.MESH

ORDERS = (("x", "y", "z"), ("y", "z", "x"), ("z", "x", "y"))
ORDER_OF = (0, 1, 2, 2)


def token_orders():
    cells = [(i, l) for i in range(LON) for l in range(LAT)]
    natural = {c: k for k, c in enumerate(cells)}
    windows = [(i, w * WIN + j) for w in range(WINDOWS) for i in range(WIN) for j in range(WIN)]
    spot = {c: k for k, c in enumerate(windows)}
    parts = []
    for north in (False, True):
        for west in (False, True):
            parts += [c for c in cells if (c[0] < HALF) == west and (c[1] < HALF) == north]
    to_window = np.zeros((TOKENS, TOKENS), np.float32)
    to_part = np.zeros_like(to_window)
    window_to_part = np.zeros_like(to_window)
    to_shifted = np.zeros_like(to_window)
    for k, c in enumerate(windows):
        to_window[k, natural[c]] = 1
    for k, c in enumerate(parts):
        to_part[k, natural[c]] = 1
        window_to_part[k, spot[c]] = 1
        to_shifted[spot[((c[0] - HALF) % LON, (c[1] - HALF) % LAT)], k] = 1
    picks = [to_window, window_to_part, to_part, to_shifted]
    picks += [to_window.T, window_to_part.T, to_shifted.T]
    return np.stack(picks)


def row_orders():
    orders = np.zeros((3, WIDTH, WIDTH), np.float32)
    for g, axes in enumerate(ORDERS):
        for place in range(WIDTH):
            at = dict(core=place // 256)
            for axis, step in zip(axes, (64, 16, 4)):
                at[axis] = place // step % 4
            lon = at["z"] % 2 * 16 + at["y"] * 4 + at["x"]
            lat = at["z"] // 2 * 2 + at["core"]
            orders[g, place, (lon * 4 + lat) * 4 + place % 4] = 1
    return orders


def mm(a, b):
    return jnp.dot(a, b, preferred_element_type=F32)


def mm_nt(a, b):
    return lax.dot_general(a, b, (((1,), (1,)), ((), ())), preferred_element_type=F32)


def mm_tn(a, b):
    return lax.dot_general(a, b, (((0,), (0,)), ((), ())), preferred_element_type=F32)


def iota(shape, dim):
    return lax.broadcasted_iota(jnp.int32, shape, dim)


def same_run(size, run):
    return (iota((size, size), 0) // run == iota((size, size), 1) // run).astype(F32).astype(BF16)


def run_sum(x, ones):
    high = x.astype(BF16)
    low = (x - high.astype(F32)).astype(BF16)
    return mm(high, ones) + mm(low, ones)


def scratch_spec():
    v = pltpu.VMEM
    return dict(
        x=v((2, TOKENS, WIDTH), BF16),
        grad=v((TOKENS, WIDTH), BF16),
        qunit=v((2, TOKENS, WIDTH), F32),
        kunit=v((2, TOKENS, WIDTH), F32),
        qinv=v((2, TOKENS, WIDTH), F32),
        kinv=v((2, TOKENS, WIDTH), F32),
        qhalf=v((2, TOKENS, WIDTH), BF16),
        khalf=v((2, TOKENS, WIDTH), BF16),
        vhalf=v((2, TOKENS, WIDTH), BF16),
        cosine=v((2, GROUPS, TOKENS, 256), F32),
        probs=v((2, GROUPS, TOKENS, 256), F32),
        attended=v((2, TOKENS, WIDTH), BF16),
        normed=v((2, TOKENS, WIDTH), F32),
        inverse=v((2, TOKENS, 1), F32),
        dz=v((TOKENS, WIDTH), BF16),
        datt=v((TOKENS, WIDTH), BF16),
        dmixed=v((TOKENS, 3 * WIDTH), BF16),
        bias=v((2, GROUPS, 64, 256), F32),
        slope=v((2, GROUPS, 64, 256), F32),
        scale=v((2, GROUPS, 1, 256), F32),
        mask=v((2, TOKENS, 256), F32),
        dtab=v((GROUPS, 64, 256), F32),
        dlog=v((GROUPS, 1, 256), F32),
        hid_out=v((TOKENS, WIDTH), BF16),
        hid_in=v((TOKENS, WIDTH), BF16),
        cot_out=v((TOKENS, WIDTH), BF16),
        cot_in=v((TOKENS, WIDTH), BF16),
        back_out=v((TOKENS, WIDTH), BF16),
        back_in=v((TOKENS, WIDTH), BF16),
        turned=v((2, PARTS, WIDTH, TOKENS), BF16),
        part=v((2, PARTS, WIDTH, WIDTH), BF16),
        r1=v((2, PARTS, 256, WIDTH), BF16),
        s1=v((2, PARTS, 256, WIDTH), BF16),
        r2=v((2, PARTS, 3, 64, WIDTH), BF16),
        s2=v((2, PARTS, 64, WIDTH), BF16),
        r3=v((2, PARTS, 3, 16, WIDTH), BF16),
        r4=v((2, PARTS, 4, 16, WIDTH), BF16),
        small=v((2, 2 * HALFROWS, 128), BF16),
        small_r1=v((2, HALFROWS, 128), BF16),
        small_x=v((2, 3, 3, 4, PIECE, 128), BF16),
        send=pltpu.SemaphoreType.DMA((168,)),
        recv=pltpu.SemaphoreType.DMA((168,)),
        load=pltpu.SemaphoreType.DMA((24,)),
        fields_v=v((TOKENS, WIDTH), BF16),
        cotangent_v=v((TOKENS, WIDTH), BF16),
        qkv_weight_v=v((2, WIDTH, 3 * WIDTH), BF16),
        proj_weight_v=v((2, WIDTH, WIDTH), BF16),
        pos_table_v=v((2, 16, 64, 64), F32),
        token_order_v=v((7, TOKENS, TOKENS), BF16),
        row_order_v=v((3, WIDTH, WIDTH), BF16),
    )


class Refs:
    pass


class Links:
    def __init__(self, r):
        self.r = r
        self.count = 0
        self.started = []
        lon, lat = lax.axis_index("lon"), lax.axis_index("lat")
        self.lon, self.lat = lon, lat
        self.core = lat % 2
        self.at = dict(x=lon % 4, y=lon // 4 % 4, z=lat // 2 * 2 + lon // 16)

    def along(self, axis, to):
        at = dict(self.at)
        at[axis] = to
        return (at["z"] % 2 * 16 + at["y"] * 4 + at["x"], at["z"] // 2 * 2 + self.core)

    def sibling(self):
        return (self.lon, self.lat // 2 * 2 + 1 - self.core)

    def shifted(self, dlon, dlat):
        return ((self.lon + dlon + 32) % 32, (self.lat + dlat + 4) % 4)

    def meet(self):
        barrier = pltpu.get_barrier_semaphore()
        others = [self.sibling()]
        for axis in ("x", "y", "z"):
            others += [self.along(axis, (self.at[axis] + d) % 4) for d in (1, 2, 3)]
        for d in (-1, 1):
            others += [self.shifted(d, 0), self.shifted(0, d), self.shifted(d, d)]
        for other in others:
            pl.semaphore_signal(barrier, inc=1, device_id=other, device_id_type=MESH)
        self.others = len(others)

    def met(self):
        pl.semaphore_wait(pltpu.get_barrier_semaphore(), self.others)

    def send(self, src, dst, to):
        k = self.count
        self.count += 1
        copy = pltpu.make_async_remote_copy(
            src_ref=src, dst_ref=dst, send_sem=self.r.send.at[k], recv_sem=self.r.recv.at[k],
            device_id=to, device_id_type=MESH,
        )
        copy.start()
        self.started.append(copy)
        return copy

    def finish(self):
        for copy in self.started:
            copy.wait_send()

    def halo(self, src, dst, sign):
        dst[0:112, :] = src[0:112, :]
        spans = ((112, 112, (sign, 0)), (224, 16, (0, sign)), (240, 16, (sign, sign)))
        return [
            self.send(src.at[pl.ds(o, n)], dst.at[pl.ds(o, n)], self.shifted(*to))
            for o, n, to in spans
        ]


class Loads:
    def __init__(self, r):
        self.r = r
        self.copies = {}

    def start(self, name, at=None):
        src, dst = getattr(self.r, name), getattr(self.r, name + "_v")
        if at is not None:
            src, dst = src.at[at], dst.at[at]
        copy = pltpu.make_async_copy(src, dst, self.r.load.at[len(self.copies)])
        copy.start()
        self.copies[name, at] = copy

    def wait(self, name, at=None):
        self.copies[name, at].wait()


def rows(at, size):
    return pl.ds(pl.multiple_of(at * size, size), size)


class Reduce:
    def __init__(self, r, links, b, g):
        self.r, self.links, self.b, self.g = r, links, b, g
        self.axes = ORDERS[ORDER_OF[g]]
        self.place = [links.at[a] for a in self.axes]
        self.step = 0

    def peers(self, level):
        axis, place = self.axes[level], self.place[level]
        return [((place + d) % 4, d) for d in (1, 2, 3)]

    def advance(self):
        r, links, b, g = self.r, self.links, self.b, self.g
        step = self.step
        self.step += 1
        if step == 0:
            src = r.part.at[b, g, rows(1 - links.core, 256)]
            self.waits = [links.send(src, r.r1.at[b, g], links.sibling())]
            return
        for copy in self.waits:
            copy.wait_recv()
        if step == 1:
            own = r.part[b, g, rows(links.core, 256), :].astype(F32)
            r.s1[b, g] = (own + r.r1[b, g].astype(F32)).astype(BF16)
            self.waits = [
                links.send(r.s1.at[b, g, rows(k, 64)], r.r2.at[b, g, d - 1], links.along(self.axes[0], k))
                for k, d in self.peers(0)
            ]
        elif step == 2:
            total = r.s1[b, g, rows(self.place[0], 64), :].astype(F32)
            for d in range(3):
                total += r.r2[b, g, d].astype(F32)
            r.s2[b, g] = total.astype(BF16)
            self.waits = [
                links.send(r.s2.at[b, g, rows(k, 16)], r.r3.at[b, g, d - 1], links.along(self.axes[1], k))
                for k, d in self.peers(1)
            ]
        elif step == 3:
            total = r.s2[b, g, rows(self.place[1], 16), :].astype(F32)
            for d in range(3):
                total += r.r3[b, g, d].astype(F32)
            mine = r.r4.at[b, g, self.place[2]]
            mine[...] = total.astype(BF16)
            self.waits = [links.send(mine, mine, links.along(self.axes[2], k)) for k, d in self.peers(2)]
        elif step == 4:
            total = r.r4[b, g, 0].astype(F32)
            for k in range(1, 4):
                total += r.r4[b, g, k].astype(F32)
            own = total[0:4, :]
            for k in range(1, 4):
                own = jnp.where(self.place[2] == k, total[4 * k : 4 * k + 4, :], own)
            if g == 3:
                r.d_proj[b] = own
            else:
                r.d_qkv[b, :, g * WIDTH : (g + 1) * WIDTH] = own


class SmallSum:
    def __init__(self, r, links, b):
        self.r, self.links, self.b = r, links, b
        self.step = 0

    def exchange(self, level, piece):
        r, links, b = self.r, self.links, self.b
        axis = ORDERS[piece][level]
        place = links.at[axis]
        mine = r.small_x.at[b, level, piece, place]
        return [links.send(mine, mine, links.along(axis, (place + d) % 4)) for d in (1, 2, 3)]

    def advance(self):
        r, links, b = self.r, self.links, self.b
        step = self.step
        self.step += 1
        half = rows(links.core, HALFROWS)
        if step == 0:
            src = r.small.at[b, rows(1 - links.core, HALFROWS)]
            self.waits = [links.send(src, r.small_r1.at[b], links.sibling())]
            return
        for copy in self.waits:
            copy.wait_recv()
        if step == 5:
            return
        self.waits = []
        for piece in range(3):
            span = slice(piece * PIECE, (piece + 1) * PIECE)
            if step == 1:
                first = r.small[b, rows(links.core * 3 + piece, PIECE), :].astype(F32)
                total = first + r.small_r1[b, span, :].astype(F32)
            else:
                total = r.small_x[b, step - 2, piece, 0].astype(F32)
                for k in range(1, 4):
                    total += r.small_x[b, step - 2, piece, k].astype(F32)
            total = total.astype(BF16)
            if step < 4:
                r.small_x[b, step - 1, piece, links.at[ORDERS[piece][step - 1]]] = total
                self.waits += self.exchange(step - 1, piece)
            else:
                r.total[b, rows(links.core * 3 + piece, PIECE), :] = total
        if step == 4:
            mine = r.total.at[b, half]
            self.waits = [links.send(mine, mine, links.sibling())]


def table_row(k):
    return k * 64 + (HALFROWS - 256) * (k // 4)


def tables(r, b):
    lane = iota((1, 256), 1) // 64
    for g in range(GROUPS):
        logs = jnp.full((1, 256), 0.0, F32) + r.log_scale[b, 4 * g]
        for h in range(1, 4):
            logs = jnp.where(lane == h, r.log_scale[b, 4 * g + h], logs)
        scale = jnp.exp(logs)
        sigma = jnp.concatenate([r.pos_table_v[b, 4 * g + h] for h in range(4)], axis=1)
        sigma = 1.0 / (1.0 + jnp.exp(-sigma))
        r.scale[b, g] = scale
        r.bias[b, g] = CAP * sigma - scale - CAP
        r.slope[b, g] = CAP * sigma * (1.0 - sigma)


def masks(r, links, b):
    shift = HALF * b
    first = r.surface[pl.ds(pl.multiple_of(links.lon * LON, LON), LON), :]
    later = r.surface[pl.ds(pl.multiple_of((links.lon + 1) % 32 * LON, LON), LON), :]
    slab = jnp.concatenate([first, later], axis=0).astype(F32).astype(BF16)

    def column(w, t):
        return (links.lat * LAT + w * WIN + t % WIN + shift) % 128

    def labels(found, col):
        return found * 2.0 + (col < shift).astype(F32)

    for w in range(WINDOWS):
        tok = iota((128, 256), 1) % 64
        pick = (iota((128, 256), 0) == column(w, tok)).astype(F32).astype(BF16)
        wide = mm(slab, pick)
        tok = iota((16, 256), 1) % 64
        found = jnp.sum(jnp.where(iota((16, 256), 0) == tok // WIN + shift, wide, 0.0), axis=0, keepdims=True)
        along = labels(found, column(w, iota((1, 256), 1) % 64))
        tok = iota((64, 128), 0)
        pick = (iota((64, 128), 1) == column(w, tok)).astype(F32).astype(BF16)
        tall = mm_nt(pick, slab)
        tok = iota((64, 16), 0)
        found = jnp.sum(jnp.where(iota((64, 16), 1) == tok // WIN + shift, tall, 0.0), axis=1, keepdims=True)
        down = labels(found, column(w, iota((64, 1), 0)))
        r.mask[b, w * 64 : w * 64 + 64, :] = (down == along).astype(F32)


def group_lanes(g, base=0):
    return pl.ds(pl.multiple_of(base + g * 128, 128), 128)


def head_lanes(dtype):
    lane = iota((1, 128), 1) // 32
    return [(lane == h).astype(F32).astype(dtype) for h in range(4)]


def expand(block, lanes):
    return jnp.concatenate([block * lanes[h] for h in range(4)], axis=0)


def collapse(block, lanes):
    return sum(block[h * 64 : h * 64 + 64, :] * lanes[h] for h in range(4))


def window(x, w):
    return x[w * 64 : w * 64 + 64, :]


def project(r, b):
    x = r.x[b]
    ones32 = same_run(256, 32)
    for name, k in (("q", 0), ("k", 1)):
        mixed = mm(x, r.qkv_weight_v[b, :, k * WIDTH : (k + 1) * WIDTH])
        square = mixed * mixed
        total = jnp.concatenate([run_sum(square[:, o : o + 256], ones32) for o in (0, 256)], axis=1)
        inv = lax.rsqrt(total + NORM_EPS)
        unit = mixed * inv
        getattr(r, name + "inv")[b] = inv
        getattr(r, name + "unit")[b] = unit
        getattr(r, name + "half")[b] = unit.astype(BF16)
    r.vhalf[b] = mm(x, r.qkv_weight_v[b, :, 2 * WIDTH : 3 * WIDTH]).astype(BF16)


def attention(r, b):
    def attend(g, carry):
        cols = group_lanes(g)
        lanes = head_lanes(BF16)
        ones64 = same_run(256, 64)
        q, k, v = r.qhalf[b, :, cols], r.khalf[b, :, cols], r.vhalf[b, :, cols]
        cosine = jnp.concatenate(
            [mm_nt(window(q, w), expand(window(k, w), lanes)) for w in range(WINDOWS)], axis=0
        )
        r.cosine[b, g] = cosine
        bias = jnp.concatenate([r.bias[b, g]] * WINDOWS, axis=0)
        expo = jnp.exp(cosine * r.scale[b, g] + bias) * r.mask[b]
        probs = expo / run_sum(expo, ones64)
        r.probs[b, g] = probs
        half = probs.astype(BF16)
        out = [mm(window(half, w), expand(window(v, w), lanes)) for w in range(WINDOWS)]
        r.attended[b, :, cols] = jnp.concatenate(out, axis=0).astype(BF16)
        return carry

    lax.fori_loop(0, GROUPS, attend, 0)


def finish_block(r, b, last):
    z = mm(r.attended[b], r.proj_weight_v[b])
    centred = z - jnp.mean(z, axis=-1, keepdims=True)
    inverse = lax.rsqrt(jnp.mean(centred * centred, axis=-1, keepdims=True) + LAYER_EPS)
    normed = centred * inverse
    r.inverse[b] = inverse
    r.normed[b] = normed
    if last:
        return None
    return (r.x[b].astype(F32) + normed * r.norm_gain[b : b + 1, :]).astype(BF16)


def backward_norm(r, b, factor):
    grad = r.grad[...].astype(F32)
    normed = r.normed[b]
    gain_term = jnp.sum(grad * normed, axis=0, keepdims=True) * factor
    row = iota((32, 128), 0)
    rest = jnp.zeros((32, 128), F32)
    for k in range(4):
        rest = jnp.where(row == k, gain_term[:, k * 128 : k * 128 + 128], rest)
    r.small[b, 256:288, :] = rest.astype(BF16)
    scaled = grad * r.norm_gain[b : b + 1, :]
    first = jnp.mean(scaled, axis=-1, keepdims=True)
    second = jnp.mean(scaled * normed, axis=-1, keepdims=True)
    dz = (r.inverse[b] * (scaled - first - normed * second)).astype(BF16)
    r.dz[...] = dz
    r.datt[...] = mm_nt(dz, r.proj_weight_v[b]).astype(BF16)


def backward_attend(r, b, begin, end):
    def attend(g, carry):
        cols = group_lanes(g)
        lanes, wide = head_lanes(BF16), head_lanes(F32)
        ones64, ones32 = same_run(256, 64), same_run(128, 32)
        q, k, v = r.qhalf[b, :, cols], r.khalf[b, :, cols], r.vhalf[b, :, cols]
        datt = r.datt[:, cols]
        probs = r.probs[b, g]
        half = probs.astype(BF16)
        dprobs = jnp.concatenate(
            [mm_nt(window(datt, w), expand(window(v, w), lanes)) for w in range(WINDOWS)], axis=0
        )
        dscores = probs * (dprobs - run_sum(probs * dprobs, ones64))
        r.dtab[g] = sum(window(dscores, w) for w in range(WINDOWS))
        r.dlog[g] = jnp.sum(dscores * r.cosine[b, g], axis=0, keepdims=True)
        dcos = (dscores * r.scale[b, g]).astype(BF16)
        dq, dk, dv = [], [], []
        for w in range(WINDOWS):
            dq.append(mm(window(dcos, w), expand(window(k, w), lanes)))
            dk.append(collapse(mm_tn(window(dcos, w), window(q, w)), wide))
            dv.append(collapse(mm_tn(window(half, w), window(datt, w)), wide))
        for base, parts, unit, inv in ((0, dq, r.qunit, r.qinv), (WIDTH, dk, r.kunit, r.kinv)):
            grad = jnp.concatenate(parts, axis=0)
            unit = unit[b, :, cols]
            grad = (grad - unit * run_sum(unit * grad, ones32)) * inv[b, :, cols]
            r.dmixed[:, group_lanes(g, base)] = grad.astype(BF16)
        r.dmixed[:, group_lanes(g, 2 * WIDTH)] = jnp.concatenate(dv, axis=0).astype(BF16)
        return carry

    lax.fori_loop(begin, end, attend, 0)


def backward_tokens(r, b):
    grad = r.grad[...].astype(F32) + mm_nt(r.dmixed[...], r.qkv_weight_v[b])
    return grad.astype(BF16)


def small_part(r, b, factor):
    ones64 = same_run(256, 64)
    row = iota((32, 128), 0)
    rest = r.small[b, 256:288, :].astype(F32)
    for g in range(GROUPS):
        term = (r.dtab[g] * r.slope[b, g] * factor).astype(BF16)
        total = run_sum(jnp.concatenate([r.dlog[g]] * 8, axis=0), ones64) * (r.scale[b, g] * factor)
        for k in range(2):
            at = table_row(2 * g + k)
            r.small[b, at : at + 64, :] = term[:, k * 128 : k * 128 + 128]
            rest = jnp.where(row == 8 + 2 * g + k, total[0:1, k * 128 : k * 128 + 128], rest)
    r.small[b, 256:288, :] = rest.astype(BF16)
    r.small[b, 544:576, :] = jnp.zeros((32, 128), BF16)


def turn(r, b, g):
    left = r.attended if g == 3 else r.x
    r.turned[b, g] = mm_nt(r.row_order_v[ORDER_OF[g]], left[b]).astype(BF16)


def weight_part(r, b, g, factor):
    right = r.dz[...] if g == 3 else r.dmixed[:, g * WIDTH : (g + 1) * WIDTH]
    r.part[b, g] = (mm(r.turned[b, g], right) * factor).astype(BF16)


INPUTS = (
    "fields", "cotangent", "surface", "qkv_weight", "proj_weight", "norm_gain", "log_scale", "pos_table",
    "token_order", "row_order",
)
OUTPUTS = ("d_fields", "d_qkv", "d_proj", "total")


def pick(order, block):
    return mm(order, block).astype(BF16)


def kernel(factor, *refs):
    r = Refs()
    for name, ref in zip(INPUTS + OUTPUTS + tuple(scratch_spec()), refs):
        setattr(r, name, ref)
    links = Links(r)
    loads = Loads(r)
    to_window, window_to_part, to_part, to_shifted, from_window, part_to_window, from_shifted = range(7)
    order = r.token_order_v
    loads.start("fields")
    loads.start("token_order")
    loads.start("qkv_weight", 0)
    loads.start("pos_table", 0)
    loads.start("cotangent")
    loads.start("proj_weight", 0)
    loads.start("row_order")
    loads.start("qkv_weight", 1)
    loads.start("pos_table", 1)
    loads.start("proj_weight", 1)
    links.meet()
    second = [Reduce(r, links, 1, g) for g in range(PARTS)]
    first = [Reduce(r, links, 0, g) for g in range(PARTS)]
    small_second, small_first = SmallSum(r, links, 1), SmallSum(r, links, 0)

    masks(r, links, 0)
    masks(r, links, 1)
    loads.wait("fields")
    loads.wait("token_order")
    r.x[0] = pick(order[to_window], r.fields_v[...])
    loads.wait("qkv_weight", 0)
    project(r, 0)
    loads.wait("pos_table", 0)
    tables(r, 0)
    attention(r, 0)
    loads.wait("cotangent")
    r.cot_out[...] = pick(order[to_part], r.cotangent_v[...])
    loads.wait("proj_weight", 0)
    links.met()
    cot = links.halo(r.cot_out, r.cot_in, -1)
    hidden = finish_block(r, 0, False)
    r.hid_out[...] = pick(order[window_to_part], hidden)
    hid = links.halo(r.hid_out, r.hid_in, -1)

    loads.wait("row_order")
    for g in range(PARTS):
        turn(r, 0, g)
    loads.wait("pos_table", 1)
    tables(r, 1)
    for copy in cot:
        copy.wait_recv()
    r.grad[...] = pick(order[to_shifted], r.cot_in[...])
    loads.wait("qkv_weight", 1)
    loads.wait("proj_weight", 1)
    for copy in hid:
        copy.wait_recv()
    r.x[1] = pick(order[to_shifted], r.hid_in[...])
    project(r, 1)
    attention(r, 1)
    finish_block(r, 1, True)
    backward_norm(r, 1, factor)
    backward_attend(r, 1, 0, GROUPS)
    r.back_out[...] = pick(order[from_shifted], backward_tokens(r, 1))
    back = links.halo(r.back_out, r.back_in, 1)

    small_part(r, 1, factor)
    small_second.advance()
    for g in range(PARTS):
        turn(r, 1, g)
        weight_part(r, 1, g, factor)
        second[g].advance()
    small_second.advance()
    for job in second:
        job.advance()
    for copy in back:
        copy.wait_recv()
    r.grad[...] = pick(order[part_to_window], r.back_in[...])
    backward_norm(r, 0, factor)
    weight_part(r, 0, 3, factor)
    first[3].advance()
    backward_attend(r, 0, 0, 2)
    first[3].advance()
    small_second.advance()
    backward_attend(r, 0, 2, 4)
    small_part(r, 0, factor)
    small_first.advance()
    for g in range(3):
        weight_part(r, 0, g, factor)
        first[g].advance()
    small_first.advance()
    for job in first[:3]:
        job.advance()
    small_second.advance()
    for job in second:
        job.advance()
    r.d_fields[...] = pick(order[from_window], backward_tokens(r, 0))
    first[3].advance()
    small_first.advance()
    for job in first[:3]:
        job.advance()
    small_second.advance()
    for job in second:
        job.advance()
    first[3].advance()
    small_first.advance()
    for job in first[:3]:
        job.advance()
    small_second.advance()
    for job in second:
        job.advance()
    small_first.advance()
    for job in first:
        job.advance()
    small_first.advance()
    links.finish()


def deliver(fields, qkv, proj, total, d_fields, d_qkv, d_proj, d_gain, d_log, d_table):
    d_fields[...] = fields[...]
    d_qkv[...] = qkv[...]
    d_proj[...] = proj[...]
    lane = iota((1, 16), 1)
    for b in range(2):
        for k in range(8):
            at = table_row(k)
            piece = total[b, at : at + 64, :].astype(F32)
            d_table[b, 2 * k] = piece[:, 0:64]
            d_table[b, 2 * k + 1] = piece[:, 64:128]
        rest = total[b, 256:272, :].astype(F32)
        for k in range(4):
            d_gain[b : b + 1, k * 128 : k * 128 + 128] = rest[k : k + 1, :]
        row = jnp.zeros((1, 16), F32)
        for h in range(16):
            spot = rest[8 + h // 2 : 9 + h // 2, h % 2 * 64 : h % 2 * 64 + 1]
            row = jnp.where(lane == h, spot, row)
        d_log[b : b + 1, :] = row


def local(fields, cotangent, surface, qkv_weight, proj_weight, norm_gain, log_scale, pos_table):
    factor = 1.0 / math.sqrt(TOKENS * 128)
    shape = jax.ShapeDtypeStruct
    orders = [jnp.asarray(x, BF16) for x in (token_orders(), row_orders())]
    vmem = pl.BlockSpec(memory_space=pltpu.VMEM)
    any_space = pl.BlockSpec(memory_space=pl.ANY)
    smem = pl.BlockSpec(memory_space=pltpu.SMEM)

    def body(*refs):
        kernel(factor, *refs)

    out = pl.pallas_call(
        body,
        out_shape=[
            shape((TOKENS, WIDTH), BF16),
            shape((2, 4, 3 * WIDTH), F32),
            shape((2, 4, WIDTH), F32),
            shape((2, 2 * HALFROWS, 128), BF16),
        ],
        in_specs=[any_space] * 2 + [vmem] + [any_space] * 2 + [vmem, smem] + [any_space] * 3,
        out_specs=[vmem] * 4,
        scratch_shapes=list(scratch_spec().values()),
        compiler_params=pltpu.CompilerParams(
            collective_id=0, has_side_effects=True, vmem_limit_bytes=60 * 1024 * 1024
        ),
    )(
        fields.reshape(TOKENS, WIDTH), cotangent.reshape(TOKENS, WIDTH), surface, qkv_weight, proj_weight,
        norm_gain, log_scale, pos_table, *orders,
    )
    out = pl.pallas_call(
        deliver,
        out_shape=[
            shape((TOKENS, WIDTH), BF16),
            shape((2, 4, 3 * WIDTH), F32),
            shape((2, 4, WIDTH), F32),
            shape((2, WIDTH), F32),
            shape((2, 16), F32),
            shape((2, 16, 64, 64), F32),
        ],
        in_specs=[vmem] * 4,
        out_specs=[vmem] * 6,
    )(*out)
    return (out[0].reshape(LON, LAT, WIDTH),) + tuple(out[1:])


def solution(mesh):
    placed = (P("lon", "lat", None), P("lon", "lat", None), P(), P(), P(), P(), P(), P())
    return jax.shard_map(
        local,
        mesh=mesh,
        in_specs=placed,
        out_specs=(
            P("lon", "lat", None),
            P(None, ("lon", "lat"), None),
            P(None, ("lon", "lat"), None),
            P(),
            P(),
            P(),
        ),
        check_vma=False,
    )
```

```python
import math

import jax
import jax.numpy as jnp
import numpy as np
from jax import lax
from jax.experimental import pallas as pl
from jax.experimental.pallas import tpu as pltpu
from jax.sharding import PartitionSpec as P

WIN = 8
HALF = WIN // 2
LON, LAT = 8, 32
TOKENS = LON * LAT
WINDOWS = 4
WIDTH = 512
GROUPS = 4
PARTS = 4
HALFROWS = 288
PIECE = 96
NORM_EPS = 1e-06
LAYER_EPS = 1e-05
CAP = 16.0
F32, BF16 = jnp.float32, jnp.bfloat16
MESH = pl.DeviceIdType.MESH

ORDERS = (("x", "y", "z"), ("y", "z", "x"), ("z", "x", "y"))
ORDER_OF = ((0, 1, 2, 0), (0, 1, 2, 1))


def token_orders():
    cells = [(i, l) for i in range(LON) for l in range(LAT)]
    natural = {c: k for k, c in enumerate(cells)}
    windows = [(i, w * WIN + j) for w in range(WINDOWS) for i in range(WIN) for j in range(WIN)]
    spot = {c: k for k, c in enumerate(windows)}
    parts = []
    for north in (False, True):
        for west in (False, True):
            parts += [c for c in cells if (c[0] < HALF) == west and (c[1] < HALF) == north]
    to_window = np.zeros((TOKENS, TOKENS), np.float32)
    to_part = np.zeros_like(to_window)
    window_to_part = np.zeros_like(to_window)
    to_shifted = np.zeros_like(to_window)
    for k, c in enumerate(windows):
        to_window[k, natural[c]] = 1
    for k, c in enumerate(parts):
        to_part[k, natural[c]] = 1
        window_to_part[k, spot[c]] = 1
        to_shifted[spot[((c[0] - HALF) % LON, (c[1] - HALF) % LAT)], k] = 1
    picks = [to_window, window_to_part, to_part, to_shifted]
    picks += [to_window.T, window_to_part.T, to_shifted.T]
    return np.stack(picks)


def row_orders():
    orders = np.zeros((3, WIDTH, WIDTH), np.float32)
    for g, axes in enumerate(ORDERS):
        for place in range(WIDTH):
            at = dict(core=place // 256)
            for axis, step in zip(axes, (64, 16, 4)):
                at[axis] = place // step % 4
            lon = at["z"] % 2 * 16 + at["y"] * 4 + at["x"]
            lat = at["z"] // 2 * 2 + at["core"]
            orders[g, place, (lon * 4 + lat) * 4 + place % 4] = 1
    return orders


def mm(a, b):
    return jnp.dot(a, b, preferred_element_type=F32)


def mm_nt(a, b):
    return lax.dot_general(a, b, (((1,), (1,)), ((), ())), preferred_element_type=F32)


def mm_tn(a, b):
    return lax.dot_general(a, b, (((0,), (0,)), ((), ())), preferred_element_type=F32)


def iota(shape, dim):
    return lax.broadcasted_iota(jnp.int32, shape, dim)


def same_run(size, run):
    return (iota((size, size), 0) // run == iota((size, size), 1) // run).astype(F32).astype(BF16)


def run_sum(x, ones):
    high = x.astype(BF16)
    low = (x - high.astype(F32)).astype(BF16)
    return mm(high, ones) + mm(low, ones)


def rough_sum(x, ones):
    return mm(x.astype(BF16), ones)


def scratch_spec():
    v = pltpu.VMEM
    return dict(
        x=v((2, TOKENS, WIDTH), BF16),
        grad=v((TOKENS, WIDTH), BF16),
        qunit=v((2, TOKENS, WIDTH), F32),
        kunit=v((2, TOKENS, WIDTH), F32),
        qinv=v((2, TOKENS, WIDTH), F32),
        kinv=v((2, TOKENS, WIDTH), F32),
        qhalf=v((2, TOKENS, WIDTH), BF16),
        khalf=v((2, TOKENS, WIDTH), BF16),
        vhalf=v((2, TOKENS, WIDTH), BF16),
        cosine=v((2, GROUPS, TOKENS, 256), F32),
        probs=v((2, GROUPS, TOKENS, 256), F32),
        attended=v((2, TOKENS, WIDTH), BF16),
        normed=v((2, TOKENS, WIDTH), F32),
        inverse=v((2, TOKENS, 1), F32),
        dz=v((TOKENS, WIDTH), BF16),
        datt=v((TOKENS, WIDTH), BF16),
        dmixed=v((TOKENS, 3 * WIDTH), BF16),
        bias=v((2, GROUPS, 64, 256), F32),
        slope=v((2, GROUPS, 64, 256), F32),
        scale=v((2, GROUPS, 1, 256), F32),
        mask=v((2, TOKENS, 256), F32),
        dcos=v((GROUPS, TOKENS, 256), BF16),
        dtab=v((GROUPS, 64, 256), F32),
        dlog=v((GROUPS, 1, 256), F32),
        hid_out=v((TOKENS, WIDTH), BF16),
        hid_in=v((TOKENS, WIDTH), BF16),
        cot_out=v((TOKENS, WIDTH), BF16),
        cot_in=v((TOKENS, WIDTH), BF16),
        back_out=v((TOKENS, WIDTH), BF16),
        back_in=v((TOKENS, WIDTH), BF16),
        turned=v((2, PARTS, WIDTH, TOKENS), BF16),
        part=v((2, PARTS, WIDTH, WIDTH), BF16),
        r1=v((2, PARTS, 256, WIDTH), BF16),
        s1=v((2, PARTS, 256, WIDTH), BF16),
        r2=v((2, PARTS, 3, 64, WIDTH), BF16),
        s2=v((2, PARTS, 16, 16, 128), BF16),
        r3=v((2, PARTS, 16, 16, 128), BF16),
        small=v((2, 2 * HALFROWS, 128), BF16),
        small_r1=v((2, HALFROWS, 128), BF16),
        small_x=v((2, 3, 3, 4, PIECE, 128), BF16),
        send=pltpu.SemaphoreType.DMA((224,)),
        recv=pltpu.SemaphoreType.DMA((224,)),
        load=pltpu.SemaphoreType.DMA((24,)),
        fields_v=v((TOKENS, WIDTH), BF16),
        cotangent_v=v((TOKENS, WIDTH), BF16),
        qkv_weight_v=v((2, WIDTH, 3 * WIDTH), BF16),
        proj_weight_v=v((2, WIDTH, WIDTH), BF16),
        pos_table_v=v((2, 16, 64, 64), F32),
        token_order_v=v((7, TOKENS, TOKENS), BF16),
        row_order_v=v((3, WIDTH, WIDTH), BF16),
    )


class Refs:
    pass


class Links:
    def __init__(self, r):
        self.r = r
        self.count = 0
        self.started = []
        lon, lat = lax.axis_index("lon"), lax.axis_index("lat")
        self.lon, self.lat = lon, lat
        self.core = lat % 2
        self.at = dict(x=lon % 4, y=lon // 4 % 4, z=lat // 2 * 2 + lon // 16)

    def along(self, axis, to, second=None, other=None):
        at = dict(self.at)
        at[axis] = to
        if second is not None:
            at[second] = other
        return (at["z"] % 2 * 16 + at["y"] * 4 + at["x"], at["z"] // 2 * 2 + self.core)

    def sibling(self):
        return (self.lon, self.lat // 2 * 2 + 1 - self.core)

    def shifted(self, dlon, dlat):
        return ((self.lon + dlon + 32) % 32, (self.lat + dlat + 4) % 4)

    def meet(self):
        barrier = pltpu.get_barrier_semaphore()
        others = [self.sibling()]
        for axis in ("x", "y", "z"):
            others += [self.along(axis, (self.at[axis] + d) % 4) for d in (1, 2, 3)]
        for a, b in (("x", "y"), ("y", "z"), ("z", "x")):
            others += [
                self.along(a, (self.at[a] + i) % 4, b, (self.at[b] + j) % 4) for i in (1, 2, 3) for j in (1, 2, 3)
            ]
        for d in (-1, 1):
            others += [self.shifted(d, 0), self.shifted(0, d), self.shifted(d, d)]
        for other in others:
            pl.semaphore_signal(barrier, inc=1, device_id=other, device_id_type=MESH)
        self.others = len(others)

    def met(self):
        pl.semaphore_wait(pltpu.get_barrier_semaphore(), self.others)

    def send(self, src, dst, to):
        k = self.count
        self.count += 1
        copy = pltpu.make_async_remote_copy(
            src_ref=src, dst_ref=dst, send_sem=self.r.send.at[k], recv_sem=self.r.recv.at[k],
            device_id=to, device_id_type=MESH,
        )
        copy.start()
        self.started.append(copy)
        return copy

    def finish(self):
        for copy in self.started:
            copy.wait_send()
        self.started = []

    def halo(self, src, dst, sign):
        dst[0:112, :] = src[0:112, :]
        spans = ((112, 112, (sign, 0)), (224, 16, (0, sign)), (240, 16, (sign, sign)))
        return [
            self.send(src.at[pl.ds(o, n)], dst.at[pl.ds(o, n)], self.shifted(*to))
            for o, n, to in spans
        ]


class Loads:
    def __init__(self, r):
        self.r = r
        self.copies = {}

    def start(self, name, at=None):
        src, dst = getattr(self.r, name), getattr(self.r, name + "_v")
        if at is not None:
            src, dst = src.at[at], dst.at[at]
        copy = pltpu.make_async_copy(src, dst, self.r.load.at[len(self.copies)])
        copy.start()
        self.copies[name, at] = copy

    def wait(self, name, at=None):
        self.copies[name, at].wait()


def rows(at, size):
    return pl.ds(pl.multiple_of(at * size, size), size)


class Reduce:
    def __init__(self, r, links, b, g):
        self.r, self.links, self.b, self.g = r, links, b, g
        self.axes = ORDERS[ORDER_OF[b][g]]
        self.place = [links.at[a] for a in self.axes]
        self.step = 0

    def peers(self, level):
        axis, place = self.axes[level], self.place[level]
        return [((place + d) % 4, d) for d in (1, 2, 3)]

    def advance(self):
        r, links, b, g = self.r, self.links, self.b, self.g
        step = self.step
        self.step += 1
        if step == 0:
            src = r.part.at[b, g, rows(1 - links.core, 256)]
            self.waits = [links.send(src, r.r1.at[b, g], links.sibling())]
            return
        for copy in self.waits:
            copy.wait_recv()
        if step == 1:
            own = r.part[b, g, rows(links.core, 256), :].astype(F32)
            r.s1[b, g] = (own + r.r1[b, g].astype(F32)).astype(BF16)
            self.waits = [
                links.send(r.s1.at[b, g, rows(k, 64)], r.r2.at[b, g, d - 1], links.along(self.axes[0], k))
                for k, d in self.peers(0)
            ]
        elif step == 2:
            total = r.s1[b, g, rows(self.place[0], 64), :].astype(F32)
            for d in range(3):
                total += r.r2[b, g, d].astype(F32)
            for chip in range(16):
                piece = total[4 * chip : 4 * chip + 4, :]
                piece = jnp.concatenate([piece[:, j * 128 : j * 128 + 128] for j in range(4)], axis=0)
                r.s2[b, g, chip] = piece.astype(BF16)
            (_, one, two), (_, i, j) = self.axes, self.place
            here = i * 4 + j
            r.r3[b, g, here] = r.s2[b, g, here]
            self.waits = []
            for d in range(1, 16):
                k, m = (i + d // 4) % 4, (j + d % 4) % 4
                self.waits.append(
                    links.send(r.s2.at[b, g, k * 4 + m], r.r3.at[b, g, here], links.along(one, k, two, m))
                )
        elif step == 3:
            total = r.r3[b, g, 0].astype(F32)
            for k in range(1, 16):
                total += r.r3[b, g, k].astype(F32)
            own = jnp.concatenate([total[4 * j : 4 * j + 4, :] for j in range(4)], axis=1)
            if g == 3:
                r.d_proj[b] = own
            else:
                r.d_qkv[b, :, g * WIDTH : (g + 1) * WIDTH] = own


class SmallSum:
    def __init__(self, r, links, b):
        self.r, self.links, self.b = r, links, b
        self.step = 0

    def exchange(self, level, piece):
        r, links, b = self.r, self.links, self.b
        axis = ORDERS[piece][level]
        place = links.at[axis]
        mine = r.small_x.at[b, level, piece, place]
        return [links.send(mine, mine, links.along(axis, (place + d) % 4)) for d in (1, 2, 3)]

    def advance(self):
        r, links, b = self.r, self.links, self.b
        step = self.step
        self.step += 1
        half = rows(links.core, HALFROWS)
        if step == 0:
            src = r.small.at[b, rows(1 - links.core, HALFROWS)]
            self.waits = [links.send(src, r.small_r1.at[b], links.sibling())]
            return
        for copy in self.waits:
            copy.wait_recv()
        if step == 5:
            return
        self.waits = []
        for piece in range(3):
            span = slice(piece * PIECE, (piece + 1) * PIECE)
            if step == 1:
                first = r.small[b, rows(links.core * 3 + piece, PIECE), :].astype(F32)
                total = first + r.small_r1[b, span, :].astype(F32)
            else:
                total = r.small_x[b, step - 2, piece, 0].astype(F32)
                for k in range(1, 4):
                    total += r.small_x[b, step - 2, piece, k].astype(F32)
            total = total.astype(BF16)
            if step < 4:
                r.small_x[b, step - 1, piece, links.at[ORDERS[piece][step - 1]]] = total
                self.waits += self.exchange(step - 1, piece)
            else:
                r.total[b, rows(links.core * 3 + piece, PIECE), :] = total
        if step == 4:
            mine = r.total.at[b, half]
            self.waits = [links.send(mine, mine, links.sibling())]


def table_row(k):
    return k * 64 + (HALFROWS - 256) * (k // 4)


def tables(r, b):
    lane = iota((1, 256), 1) // 64
    for g in range(GROUPS):
        logs = jnp.full((1, 256), 0.0, F32) + r.log_scale[b, 4 * g]
        for h in range(1, 4):
            logs = jnp.where(lane == h, r.log_scale[b, 4 * g + h], logs)
        scale = jnp.exp(logs)
        sigma = jnp.concatenate([r.pos_table_v[b, 4 * g + h] for h in range(4)], axis=1)
        sigma = 1.0 / (1.0 + jnp.exp(-sigma))
        r.scale[b, g] = scale
        r.bias[b, g] = CAP * sigma - scale - CAP
        r.slope[b, g] = CAP * sigma * (1.0 - sigma)


def masks(r, links, b):
    shift = HALF * b
    first = r.surface[pl.ds(pl.multiple_of(links.lon * LON, LON), LON), :]
    later = r.surface[pl.ds(pl.multiple_of((links.lon + 1) % 32 * LON, LON), LON), :]
    slab = jnp.concatenate([first, later], axis=0).astype(F32).astype(BF16)

    def column(w, t):
        return (links.lat * LAT + w * WIN + t % WIN + shift) % 128

    def labels(found, col):
        return found * 2.0 + (col < shift).astype(F32)

    for w in range(WINDOWS):
        tok = iota((128, 256), 1) % 64
        pick = (iota((128, 256), 0) == column(w, tok)).astype(F32).astype(BF16)
        wide = mm(slab, pick)
        tok = iota((16, 256), 1) % 64
        found = jnp.sum(jnp.where(iota((16, 256), 0) == tok // WIN + shift, wide, 0.0), axis=0, keepdims=True)
        along = labels(found, column(w, iota((1, 256), 1) % 64))
        tok = iota((64, 128), 0)
        pick = (iota((64, 128), 1) == column(w, tok)).astype(F32).astype(BF16)
        tall = mm_nt(pick, slab)
        tok = iota((64, 16), 0)
        found = jnp.sum(jnp.where(iota((64, 16), 1) == tok // WIN + shift, tall, 0.0), axis=1, keepdims=True)
        down = labels(found, column(w, iota((64, 1), 0)))
        r.mask[b, w * 64 : w * 64 + 64, :] = (down == along).astype(F32)


def group_lanes(g, base=0):
    return pl.ds(pl.multiple_of(base + g * 128, 128), 128)


def head_lanes(dtype):
    lane = iota((1, 128), 1) // 32
    return [(lane == h).astype(F32).astype(dtype) for h in range(4)]


def expand(block, lanes):
    return jnp.concatenate([block * lanes[h] for h in range(4)], axis=0)


def collapse(block, lanes):
    return sum(block[h * 64 : h * 64 + 64, :] * lanes[h] for h in range(4))


def window(x, w):
    return x[w * 64 : w * 64 + 64, :]


def project(r, b):
    x = r.x[b]
    ones32 = same_run(256, 32)
    for name, k in (("q", 0), ("k", 1)):
        mixed = mm(x, r.qkv_weight_v[b, :, k * WIDTH : (k + 1) * WIDTH])
        square = mixed * mixed
        total = jnp.concatenate([rough_sum(square[:, o : o + 256], ones32) for o in (0, 256)], axis=1)
        inv = lax.rsqrt(total + NORM_EPS)
        unit = mixed * inv
        getattr(r, name + "inv")[b] = inv
        getattr(r, name + "unit")[b] = unit
        getattr(r, name + "half")[b] = unit.astype(BF16)
    r.vhalf[b] = mm(x, r.qkv_weight_v[b, :, 2 * WIDTH : 3 * WIDTH]).astype(BF16)


def attention(r, b):
    def attend(g):
        cols = group_lanes(g)
        lanes = head_lanes(BF16)
        ones64 = same_run(256, 64)
        q, k, v = r.qhalf[b, :, cols], r.khalf[b, :, cols], r.vhalf[b, :, cols]
        cosine = jnp.concatenate(
            [mm_nt(window(q, w), expand(window(k, w), lanes)) for w in range(WINDOWS)], axis=0
        )
        r.cosine[b, g] = cosine
        bias = jnp.concatenate([r.bias[b, g]] * WINDOWS, axis=0)
        expo = jnp.exp(cosine * r.scale[b, g] + bias) * r.mask[b]
        probs = expo / run_sum(expo, ones64)
        r.probs[b, g] = probs
        half = probs.astype(BF16)
        out = [mm(window(half, w), expand(window(v, w), lanes)) for w in range(WINDOWS)]
        r.attended[b, :, cols] = jnp.concatenate(out, axis=0).astype(BF16)

    for g in range(GROUPS):
        attend(g)


def finish_block(r, b, last):
    z = mm(r.attended[b], r.proj_weight_v[b])
    centred = z - jnp.mean(z, axis=-1, keepdims=True)
    inverse = lax.rsqrt(jnp.mean(centred * centred, axis=-1, keepdims=True) + LAYER_EPS)
    normed = centred * inverse
    r.inverse[b] = inverse
    r.normed[b] = normed
    if last:
        return None
    return (r.x[b].astype(F32) + normed * r.norm_gain[b : b + 1, :]).astype(BF16)


def backward_norm(r, b, factor):
    grad = r.grad[...].astype(F32)
    normed = r.normed[b]
    gain_term = jnp.sum(grad * normed, axis=0, keepdims=True) * factor
    row = iota((32, 128), 0)
    rest = jnp.zeros((32, 128), F32)
    for k in range(4):
        rest = jnp.where(row == k, gain_term[:, k * 128 : k * 128 + 128], rest)
    r.small[b, 256:288, :] = rest.astype(BF16)
    scaled = grad * r.norm_gain[b : b + 1, :]
    first = jnp.mean(scaled, axis=-1, keepdims=True)
    second = jnp.mean(scaled * normed, axis=-1, keepdims=True)
    dz = (r.inverse[b] * (scaled - first - normed * second)).astype(BF16)
    r.dz[...] = dz
    r.datt[...] = mm_nt(dz, r.proj_weight_v[b]).astype(BF16)


def backward_values(r, b):
    wide = head_lanes(F32)
    for g in range(GROUPS):
        cols = group_lanes(g)
        half, datt = r.probs[b, g].astype(BF16), r.datt[:, cols]
        dv = [collapse(mm_tn(window(half, w), window(datt, w)), wide) for w in range(WINDOWS)]
        r.dmixed[:, group_lanes(g, 2 * WIDTH)] = jnp.concatenate(dv, axis=0).astype(BF16)


def backward_scores(r, b):
    lanes = head_lanes(BF16)
    ones64 = same_run(256, 64)
    for g in range(GROUPS):
        cols = group_lanes(g)
        v, datt, probs = r.vhalf[b, :, cols], r.datt[:, cols], r.probs[b, g]
        dprobs = jnp.concatenate(
            [mm_nt(window(datt, w), expand(window(v, w), lanes)) for w in range(WINDOWS)], axis=0
        )
        dscores = probs * (dprobs - run_sum(probs * dprobs, ones64))
        r.dtab[g] = sum(window(dscores, w) for w in range(WINDOWS))
        r.dlog[g] = jnp.sum(dscores * r.cosine[b, g], axis=0, keepdims=True)
        r.dcos[g] = (dscores * r.scale[b, g]).astype(BF16)


def backward_keys(r, b, begin, end):
    lanes, wide = head_lanes(BF16), head_lanes(F32)
    ones32 = same_run(128, 32)
    for g in range(begin, end):
        cols = group_lanes(g)
        q, k, dcos = r.qhalf[b, :, cols], r.khalf[b, :, cols], r.dcos[g]
        dq, dk = [], []
        for w in range(WINDOWS):
            dq.append(mm(window(dcos, w), expand(window(k, w), lanes)))
            dk.append(collapse(mm_tn(window(dcos, w), window(q, w)), wide))
        for base, parts, unit, inv in ((0, dq, r.qunit, r.qinv), (WIDTH, dk, r.kunit, r.kinv)):
            grad = jnp.concatenate(parts, axis=0)
            unit = unit[b, :, cols]
            grad = (grad - unit * rough_sum(unit * grad, ones32)) * inv[b, :, cols]
            r.dmixed[:, group_lanes(g, base)] = grad.astype(BF16)


def backward_tokens(r, b):
    grad = r.grad[...].astype(F32) + mm_nt(r.dmixed[...], r.qkv_weight_v[b])
    return grad.astype(BF16)


def small_part(r, b, factor):
    ones64 = same_run(256, 64)
    row = iota((32, 128), 0)
    rest = r.small[b, 256:288, :].astype(F32)
    for g in range(GROUPS):
        term = (r.dtab[g] * r.slope[b, g] * factor).astype(BF16)
        total = run_sum(jnp.concatenate([r.dlog[g]] * 8, axis=0), ones64) * (r.scale[b, g] * factor)
        for k in range(2):
            at = table_row(2 * g + k)
            r.small[b, at : at + 64, :] = term[:, k * 128 : k * 128 + 128]
            rest = jnp.where(row == 8 + 2 * g + k, total[0:1, k * 128 : k * 128 + 128], rest)
    r.small[b, 256:288, :] = rest.astype(BF16)
    r.small[b, 544:576, :] = jnp.zeros((32, 128), BF16)


def turn(r, b, g):
    left = r.attended if g == 3 else r.x
    r.turned[b, g] = mm_nt(r.row_order_v[ORDER_OF[b][g]], left[b]).astype(BF16)


def weight_part(r, b, g, factor):
    right = r.dz[...] if g == 3 else r.dmixed[:, g * WIDTH : (g + 1) * WIDTH]
    r.part[b, g] = (mm(r.turned[b, g], right) * factor).astype(BF16)


INPUTS = (
    "fields", "cotangent", "surface", "qkv_weight", "proj_weight", "norm_gain", "log_scale", "pos_table",
    "token_order", "row_order",
)
OUTPUTS = ("d_fields", "d_qkv", "d_proj", "total")


def pick(order, block):
    return mm(order, block).astype(BF16)


def kernel(factor, *refs):
    r = Refs()
    for name, ref in zip(INPUTS + OUTPUTS + tuple(scratch_spec()), refs):
        setattr(r, name, ref)
    links = Links(r)
    loads = Loads(r)
    to_window, window_to_part, to_part, to_shifted, from_window, part_to_window, from_shifted = range(7)
    order = r.token_order_v
    loads.start("fields")
    loads.start("token_order")
    loads.start("qkv_weight", 0)
    loads.start("pos_table", 0)
    loads.start("cotangent")
    loads.start("proj_weight", 0)
    loads.start("row_order")
    loads.start("qkv_weight", 1)
    loads.start("pos_table", 1)
    loads.start("proj_weight", 1)
    links.meet()
    second = [Reduce(r, links, 1, g) for g in range(PARTS)]
    first = [Reduce(r, links, 0, g) for g in range(PARTS)]
    small_second, small_first = SmallSum(r, links, 1), SmallSum(r, links, 0)

    masks(r, links, 0)
    loads.wait("fields")
    loads.wait("token_order")
    r.x[0] = pick(order[to_window], r.fields_v[...])
    loads.wait("qkv_weight", 0)
    project(r, 0)
    loads.wait("pos_table", 0)
    tables(r, 0)
    attention(r, 0)
    loads.wait("proj_weight", 0)
    hidden = finish_block(r, 0, False)
    r.hid_out[...] = pick(order[window_to_part], hidden)
    links.met()
    hid = links.halo(r.hid_out, r.hid_in, -1)
    loads.wait("cotangent")
    r.cot_out[...] = pick(order[to_part], r.cotangent_v[...])
    cot = links.halo(r.cot_out, r.cot_in, -1)
    masks(r, links, 1)
    loads.wait("pos_table", 1)
    tables(r, 1)
    loads.wait("row_order")
    for g in range(PARTS):
        turn(r, 0, g)
    loads.wait("qkv_weight", 1)
    loads.wait("proj_weight", 1)
    for copy in hid:
        copy.wait_recv()
    r.x[1] = pick(order[to_shifted], r.hid_in[...])
    project(r, 1)
    attention(r, 1)
    finish_block(r, 1, True)
    for copy in cot:
        copy.wait_recv()
    r.grad[...] = pick(order[to_shifted], r.cot_in[...])
    backward_norm(r, 1, factor)
    backward_values(r, 1)
    backward_scores(r, 1)
    small_part(r, 1, factor)
    small_second.advance()
    backward_keys(r, 1, 0, GROUPS)
    r.back_out[...] = pick(order[from_shifted], backward_tokens(r, 1))
    back = links.halo(r.back_out, r.back_in, 1)

    small_second.advance()
    for g in (3, 2, 1, 0):
        turn(r, 1, g)
        weight_part(r, 1, g, factor)
        second[g].advance()
    for g in (3, 2, 1):
        second[g].advance()
    for copy in back:
        copy.wait_recv()
    second[0].advance()
    r.grad[...] = pick(order[part_to_window], r.back_in[...])
    backward_norm(r, 0, factor)
    weight_part(r, 0, 3, factor)
    first[3].advance()
    backward_values(r, 0)
    weight_part(r, 0, 2, factor)
    first[2].advance()
    first[3].advance()
    backward_scores(r, 0)
    small_part(r, 0, factor)
    small_first.advance()
    first[2].advance()
    backward_keys(r, 0, 0, 2)
    small_first.advance()
    backward_keys(r, 0, 2, 4)
    for g in (0, 1):
        weight_part(r, 0, g, factor)
        first[g].advance()
    small_second.advance()
    first[0].advance()
    first[1].advance()
    for job in second:
        job.advance()
    r.d_fields[...] = pick(order[from_window], backward_tokens(r, 0))
    small_first.advance()
    small_second.advance()
    first[3].advance()
    first[2].advance()
    for job in second:
        job.advance()
    small_first.advance()
    first[0].advance()
    first[1].advance()
    small_second.advance()
    links.finish()
    small_second.advance()
    first[3].advance()
    small_first.advance()
    for job in first[:3]:
        job.advance()
    small_first.advance()
    links.finish()


def deliver(fields, qkv, proj, total, d_fields, d_qkv, d_proj, d_gain, d_log, d_table):
    d_fields[...] = fields[...]
    d_qkv[...] = qkv[...]
    d_proj[...] = proj[...]
    lane = iota((1, 16), 1)
    for b in range(2):
        for k in range(8):
            at = table_row(k)
            piece = total[b, at : at + 64, :].astype(F32)
            d_table[b, 2 * k] = piece[:, 0:64]
            d_table[b, 2 * k + 1] = piece[:, 64:128]
        rest = total[b, 256:272, :].astype(F32)
        for k in range(4):
            d_gain[b : b + 1, k * 128 : k * 128 + 128] = rest[k : k + 1, :]
        row = jnp.zeros((1, 16), F32)
        for h in range(16):
            spot = rest[8 + h // 2 : 9 + h // 2, h % 2 * 64 : h % 2 * 64 + 1]
            row = jnp.where(lane == h, spot, row)
        d_log[b : b + 1, :] = row


def local(fields, cotangent, surface, qkv_weight, proj_weight, norm_gain, log_scale, pos_table):
    factor = 1.0 / math.sqrt(TOKENS * 128)
    shape = jax.ShapeDtypeStruct
    orders = [jnp.asarray(x, BF16) for x in (token_orders(), row_orders())]
    vmem = pl.BlockSpec(memory_space=pltpu.VMEM)
    any_space = pl.BlockSpec(memory_space=pl.ANY)
    smem = pl.BlockSpec(memory_space=pltpu.SMEM)

    def body(*refs):
        kernel(factor, *refs)

    out = pl.pallas_call(
        body,
        out_shape=[
            shape((TOKENS, WIDTH), BF16),
            shape((2, 4, 3 * WIDTH), F32),
            shape((2, 4, WIDTH), F32),
            shape((2, 2 * HALFROWS, 128), BF16),
        ],
        in_specs=[any_space] * 2 + [vmem] + [any_space] * 2 + [vmem, smem] + [any_space] * 3,
        out_specs=[vmem] * 4,
        scratch_shapes=list(scratch_spec().values()),
        compiler_params=pltpu.CompilerParams(
            collective_id=0, has_side_effects=True, vmem_limit_bytes=60 * 1024 * 1024
        ),
    )(
        fields.reshape(TOKENS, WIDTH), cotangent.reshape(TOKENS, WIDTH), surface, qkv_weight, proj_weight,
        norm_gain, log_scale, pos_table, *orders,
    )
    out = pl.pallas_call(
        deliver,
        out_shape=[
            shape((TOKENS, WIDTH), BF16),
            shape((2, 4, 3 * WIDTH), F32),
            shape((2, 4, WIDTH), F32),
            shape((2, WIDTH), F32),
            shape((2, 16), F32),
            shape((2, 16, 64, 64), F32),
        ],
        in_specs=[vmem] * 4,
        out_specs=[vmem] * 6,
    )(*out)
    return (out[0].reshape(LON, LAT, WIDTH),) + tuple(out[1:])


def solution(mesh):
    placed = (P("lon", "lat", None), P("lon", "lat", None), P(), P(), P(), P(), P(), P())
    return jax.shard_map(
        local,
        mesh=mesh,
        in_specs=placed,
        out_specs=(
            P("lon", "lat", None),
            P(None, ("lon", "lat"), None),
            P(None, ("lon", "lat"), None),
            P(),
            P(),
            P(),
        ),
        check_vma=False,
    )
```

```python
import math

import jax
import jax.numpy as jnp
import numpy as np
from jax import lax
from jax.experimental import pallas as pl
from jax.experimental.pallas import tpu as pltpu
from jax.sharding import PartitionSpec as P

WIN = 8
HALF = WIN // 2
LON, LAT = 8, 32
TOKENS = LON * LAT
WINDOWS = 4
WIDTH = 512
GROUPS = 4
PARTS = 4
HALFROWS = 288
PIECE = 96
NORM_EPS = 1e-06
LAYER_EPS = 1e-05
CAP = 16.0
F32, BF16 = jnp.float32, jnp.bfloat16
MESH = pl.DeviceIdType.MESH

SPANS = (((0, 48), (112, 48), (224, 16), (240, 16)), ((48, 64), (160, 64)))
SHIFTED_SPANS = (((0, 64), (112, 64)), ((64, 48), (176, 48), (224, 16), (240, 16)))

ORDERS = (("x", "y", "z"), ("y", "z", "x"), ("z", "x", "y"))
ORDER_OF = ((0, 1, 2, 0), (0, 1, 2, 1))


def token_orders():
    cells = [(i, l) for i in range(LON) for l in range(LAT)]
    natural = {c: k for k, c in enumerate(cells)}
    windows = [(i, w * WIN + j) for w in range(WINDOWS) for i in range(WIN) for j in range(WIN)]
    spot = {c: k for k, c in enumerate(windows)}
    parts = []
    for north in (False, True):
        for west in (False, True):
            part = [c for c in cells if (c[0] < HALF) == west and (c[1] < HALF) == north]
            parts += sorted(part, key=lambda c: ((c[1] >= 16) + (c[1] >= 20), c))
    to_window = np.zeros((TOKENS, TOKENS), np.float32)
    to_part = np.zeros_like(to_window)
    window_to_part = np.zeros_like(to_window)
    to_shifted = np.zeros_like(to_window)
    for k, c in enumerate(windows):
        to_window[k, natural[c]] = 1
    for k, c in enumerate(parts):
        to_part[k, natural[c]] = 1
        window_to_part[k, spot[c]] = 1
        to_shifted[spot[((c[0] - HALF) % LON, (c[1] - HALF) % LAT)], k] = 1
    picks = [to_window, window_to_part, to_part, to_shifted]
    picks += [to_window.T, window_to_part.T, to_shifted.T]
    return np.stack(picks)


def row_orders():
    orders = np.zeros((3, WIDTH, WIDTH), np.float32)
    for g, axes in enumerate(ORDERS):
        for place in range(WIDTH):
            at = dict(core=place // 256)
            for axis, step in zip(axes, (64, 16, 4)):
                at[axis] = place // step % 4
            lon = at["z"] % 2 * 16 + at["y"] * 4 + at["x"]
            lat = at["z"] // 2 * 2 + at["core"]
            orders[g, place, (lon * 4 + lat) * 4 + place % 4] = 1
    return orders


def mm(a, b):
    return jnp.dot(a, b, preferred_element_type=F32)


def mm_nt(a, b):
    return lax.dot_general(a, b, (((1,), (1,)), ((), ())), preferred_element_type=F32)


def mm_tn(a, b):
    return lax.dot_general(a, b, (((0,), (0,)), ((), ())), preferred_element_type=F32)


def iota(shape, dim):
    return lax.broadcasted_iota(jnp.int32, shape, dim)


def same_run(size, run):
    return (iota((size, size), 0) // run == iota((size, size), 1) // run).astype(F32).astype(BF16)


def run_sum(x, ones):
    high = x.astype(BF16)
    low = (x - high.astype(F32)).astype(BF16)
    return mm(high, ones) + mm(low, ones)


def rough_sum(x, ones):
    return mm(x.astype(BF16), ones)


def scratch_spec():
    v = pltpu.VMEM
    return dict(
        x=v((2, TOKENS, WIDTH), BF16),
        grad=v((TOKENS, WIDTH), BF16),
        qunit=v((2, TOKENS, WIDTH), F32),
        kunit=v((2, TOKENS, WIDTH), F32),
        qinv=v((2, TOKENS, WIDTH), F32),
        kinv=v((2, TOKENS, WIDTH), F32),
        qhalf=v((2, TOKENS, WIDTH), BF16),
        khalf=v((2, TOKENS, WIDTH), BF16),
        vhalf=v((2, TOKENS, WIDTH), BF16),
        cosine=v((2, GROUPS, TOKENS, 256), F32),
        probs=v((2, GROUPS, TOKENS, 256), F32),
        attended=v((2, TOKENS, WIDTH), BF16),
        normed=v((2, TOKENS, WIDTH), F32),
        inverse=v((2, TOKENS, 1), F32),
        dz=v((TOKENS, WIDTH), BF16),
        datt=v((TOKENS, WIDTH), BF16),
        dmixed=v((TOKENS, 3 * WIDTH), BF16),
        bias=v((2, GROUPS, 64, 256), F32),
        slope=v((2, GROUPS, 64, 256), F32),
        scale=v((2, GROUPS, 1, 256), F32),
        mask=v((2, TOKENS, 256), F32),
        dcos=v((GROUPS, TOKENS, 256), BF16),
        dtab=v((GROUPS, 64, 256), F32),
        dlog=v((GROUPS, 1, 256), F32),
        hid_out=v((TOKENS, WIDTH), BF16),
        hid_in=v((TOKENS, WIDTH), BF16),
        cot_out=v((TOKENS, WIDTH), BF16),
        cot_in=v((TOKENS, WIDTH), BF16),
        back_out=v((TOKENS, WIDTH), BF16),
        back_in=v((TOKENS, WIDTH), BF16),
        turned=v((2, PARTS, WIDTH, TOKENS), BF16),
        part=v((2, PARTS, WIDTH, WIDTH), BF16),
        r1=v((2, PARTS, 256, WIDTH), BF16),
        s1=v((2, PARTS, 256, WIDTH), BF16),
        r2=v((2, PARTS, 3, 64, WIDTH), BF16),
        s2=v((2, PARTS, 16, 16, 128), BF16),
        r3=v((2, PARTS, 16, 16, 128), BF16),
        small=v((2, 2 * HALFROWS, 128), BF16),
        small_r1=v((2, HALFROWS, 128), BF16),
        small_x=v((2, 3, 3, 4, PIECE, 128), BF16),
        send=pltpu.SemaphoreType.DMA((224,)),
        recv=pltpu.SemaphoreType.DMA((224,)),
        load=pltpu.SemaphoreType.DMA((24,)),
        fields_v=v((TOKENS, WIDTH), BF16),
        cotangent_v=v((TOKENS, WIDTH), BF16),
        qkv_weight_v=v((2, WIDTH, 3 * WIDTH), BF16),
        proj_weight_v=v((2, WIDTH, WIDTH), BF16),
        pos_table_v=v((2, 16, 64, 64), F32),
        token_order_v=v((7, TOKENS, TOKENS), BF16),
        row_order_v=v((3, WIDTH, WIDTH), BF16),
    )


class Refs:
    pass


class Links:
    def __init__(self, r):
        self.r = r
        self.count = 0
        self.started = []
        lon, lat = lax.axis_index("lon"), lax.axis_index("lat")
        self.lon, self.lat = lon, lat
        self.core = lat % 2
        self.at = dict(x=lon % 4, y=lon // 4 % 4, z=lat // 2 * 2 + lon // 16)

    def along(self, axis, to, second=None, other=None):
        at = dict(self.at)
        at[axis] = to
        if second is not None:
            at[second] = other
        return (at["z"] % 2 * 16 + at["y"] * 4 + at["x"], at["z"] // 2 * 2 + self.core)

    def sibling(self):
        return (self.lon, self.lat // 2 * 2 + 1 - self.core)

    def shifted(self, dlon, dlat):
        return ((self.lon + dlon + 32) % 32, (self.lat + dlat + 4) % 4)

    def meet(self):
        barrier = pltpu.get_barrier_semaphore()
        others = [self.sibling()]
        for axis in ("x", "y", "z"):
            others += [self.along(axis, (self.at[axis] + d) % 4) for d in (1, 2, 3)]
        for a, b in (("x", "y"), ("y", "z"), ("z", "x")):
            others += [
                self.along(a, (self.at[a] + i) % 4, b, (self.at[b] + j) % 4) for i in (1, 2, 3) for j in (1, 2, 3)
            ]
        for d in (-1, 1):
            others += [self.shifted(d, 0), self.shifted(0, d), self.shifted(d, d)]
        for other in others:
            pl.semaphore_signal(barrier, inc=1, device_id=other, device_id_type=MESH)
        self.others = len(others)

    def met(self):
        pl.semaphore_wait(pltpu.get_barrier_semaphore(), self.others)

    def send(self, src, dst, to):
        k = self.count
        self.count += 1
        copy = pltpu.make_async_remote_copy(
            src_ref=src, dst_ref=dst, send_sem=self.r.send.at[k], recv_sem=self.r.recv.at[k],
            device_id=to, device_id_type=MESH,
        )
        copy.start()
        self.started.append(copy)
        return copy

    def finish(self):
        for copy in self.started:
            copy.wait_send()
        self.started = []

    def halo(self, src, dst, sign, spans):
        copies = []
        for first, count in spans:
            if first < 112:
                dst[first : first + count, :] = src[first : first + count, :]
                continue
            to = (sign, 0) if first < 224 else ((0, sign) if first < 240 else (sign, sign))
            copies.append(self.send(src.at[pl.ds(first, count)], dst.at[pl.ds(first, count)], self.shifted(*to)))
        return copies


class Loads:
    def __init__(self, r):
        self.r = r
        self.copies = {}

    def start(self, name, at=None):
        src, dst = getattr(self.r, name), getattr(self.r, name + "_v")
        if at is not None:
            src, dst = src.at[at], dst.at[at]
        copy = pltpu.make_async_copy(src, dst, self.r.load.at[len(self.copies)])
        copy.start()
        self.copies[name, at] = copy

    def wait(self, name, at=None):
        self.copies[name, at].wait()


def rows(at, size):
    return pl.ds(pl.multiple_of(at * size, size), size)


class Reduce:
    def __init__(self, r, links, b, g):
        self.r, self.links, self.b, self.g = r, links, b, g
        self.axes = ORDERS[ORDER_OF[b][g]]
        self.place = [links.at[a] for a in self.axes]
        self.step = 0

    def peers(self, level):
        axis, place = self.axes[level], self.place[level]
        return [((place + d) % 4, d) for d in (1, 2, 3)]

    def advance(self):
        r, links, b, g = self.r, self.links, self.b, self.g
        step = self.step
        self.step += 1
        if step == 0:
            src = r.part.at[b, g, rows(1 - links.core, 256)]
            self.waits = [links.send(src, r.r1.at[b, g], links.sibling())]
            return
        for copy in self.waits:
            copy.wait_recv()
        if step == 1:
            own = r.part[b, g, rows(links.core, 256), :].astype(F32)
            r.s1[b, g] = (own + r.r1[b, g].astype(F32)).astype(BF16)
            self.waits = [
                links.send(r.s1.at[b, g, rows(k, 64)], r.r2.at[b, g, d - 1], links.along(self.axes[0], k))
                for k, d in self.peers(0)
            ]
        elif step == 2:
            total = r.s1[b, g, rows(self.place[0], 64), :].astype(F32)
            for d in range(3):
                total += r.r2[b, g, d].astype(F32)
            for chip in range(16):
                piece = total[4 * chip : 4 * chip + 4, :]
                piece = jnp.concatenate([piece[:, j * 128 : j * 128 + 128] for j in range(4)], axis=0)
                r.s2[b, g, chip] = piece.astype(BF16)
            (_, one, two), (_, i, j) = self.axes, self.place
            here = i * 4 + j
            r.r3[b, g, here] = r.s2[b, g, here]
            self.waits = []
            for d in range(1, 16):
                k, m = (i + d // 4) % 4, (j + d % 4) % 4
                self.waits.append(
                    links.send(r.s2.at[b, g, k * 4 + m], r.r3.at[b, g, here], links.along(one, k, two, m))
                )
        elif step == 3:
            total = r.r3[b, g, 0].astype(F32)
            for k in range(1, 16):
                total += r.r3[b, g, k].astype(F32)
            own = jnp.concatenate([total[4 * j : 4 * j + 4, :] for j in range(4)], axis=1)
            if g == 3:
                r.d_proj[b] = own
            else:
                r.d_qkv[b, :, g * WIDTH : (g + 1) * WIDTH] = own


class SmallSum:
    def __init__(self, r, links, b):
        self.r, self.links, self.b = r, links, b
        self.step = 0

    def exchange(self, level, piece):
        r, links, b = self.r, self.links, self.b
        axis = ORDERS[piece][level]
        place = links.at[axis]
        mine = r.small_x.at[b, level, piece, place]
        return [links.send(mine, mine, links.along(axis, (place + d) % 4)) for d in (1, 2, 3)]

    def advance(self):
        r, links, b = self.r, self.links, self.b
        step = self.step
        self.step += 1
        half = rows(links.core, HALFROWS)
        if step == 0:
            src = r.small.at[b, rows(1 - links.core, HALFROWS)]
            self.waits = [links.send(src, r.small_r1.at[b], links.sibling())]
            return
        for copy in self.waits:
            copy.wait_recv()
        if step == 5:
            return
        self.waits = []
        for piece in range(3):
            span = slice(piece * PIECE, (piece + 1) * PIECE)
            if step == 1:
                first = r.small[b, rows(links.core * 3 + piece, PIECE), :].astype(F32)
                total = first + r.small_r1[b, span, :].astype(F32)
            else:
                total = r.small_x[b, step - 2, piece, 0].astype(F32)
                for k in range(1, 4):
                    total += r.small_x[b, step - 2, piece, k].astype(F32)
            total = total.astype(BF16)
            if step < 4:
                r.small_x[b, step - 1, piece, links.at[ORDERS[piece][step - 1]]] = total
                self.waits += self.exchange(step - 1, piece)
            else:
                r.total[b, rows(links.core * 3 + piece, PIECE), :] = total
        if step == 4:
            mine = r.total.at[b, half]
            self.waits = [links.send(mine, mine, links.sibling())]


def table_row(k):
    return k * 64 + (HALFROWS - 256) * (k // 4)


def tables(r, b):
    lane = iota((1, 256), 1) // 64
    for g in range(GROUPS):
        logs = jnp.full((1, 256), 0.0, F32) + r.log_scale[b, 4 * g]
        for h in range(1, 4):
            logs = jnp.where(lane == h, r.log_scale[b, 4 * g + h], logs)
        scale = jnp.exp(logs)
        sigma = jnp.concatenate([r.pos_table_v[b, 4 * g + h] for h in range(4)], axis=1)
        sigma = 1.0 / (1.0 + jnp.exp(-sigma))
        r.scale[b, g] = scale
        r.bias[b, g] = CAP * sigma - scale - CAP
        r.slope[b, g] = CAP * sigma * (1.0 - sigma)


def masks(r, links, b):
    shift = HALF * b
    first = r.surface[pl.ds(pl.multiple_of(links.lon * LON, LON), LON), :]
    later = r.surface[pl.ds(pl.multiple_of((links.lon + 1) % 32 * LON, LON), LON), :]
    slab = jnp.concatenate([first, later], axis=0).astype(F32).astype(BF16)

    def column(w, t):
        return (links.lat * LAT + w * WIN + t % WIN + shift) % 128

    def labels(found, col):
        return found * 2.0 + (col < shift).astype(F32)

    for w in range(WINDOWS):
        tok = iota((128, 256), 1) % 64
        pick = (iota((128, 256), 0) == column(w, tok)).astype(F32).astype(BF16)
        wide = mm(slab, pick)
        tok = iota((16, 256), 1) % 64
        found = jnp.sum(jnp.where(iota((16, 256), 0) == tok // WIN + shift, wide, 0.0), axis=0, keepdims=True)
        along = labels(found, column(w, iota((1, 256), 1) % 64))
        tok = iota((64, 128), 0)
        pick = (iota((64, 128), 1) == column(w, tok)).astype(F32).astype(BF16)
        tall = mm_nt(pick, slab)
        tok = iota((64, 16), 0)
        found = jnp.sum(jnp.where(iota((64, 16), 1) == tok // WIN + shift, tall, 0.0), axis=1, keepdims=True)
        down = labels(found, column(w, iota((64, 1), 0)))
        r.mask[b, w * 64 : w * 64 + 64, :] = (down == along).astype(F32)


def group_lanes(g, base=0):
    return pl.ds(pl.multiple_of(base + g * 128, 128), 128)


def head_lanes(dtype):
    lane = iota((1, 128), 1) // 32
    return [(lane == h).astype(F32).astype(dtype) for h in range(4)]


def expand(block, lanes):
    return jnp.concatenate([block * lanes[h] for h in range(4)], axis=0)


def collapse(block, lanes):
    return sum(block[h * 64 : h * 64 + 64, :] * lanes[h] for h in range(4))


def window(x, w):
    return x[w * 64 : w * 64 + 64, :]


def project(r, b):
    x = r.x[b]
    ones32 = same_run(256, 32)
    for name, k in (("q", 0), ("k", 1)):
        mixed = mm(x, r.qkv_weight_v[b, :, k * WIDTH : (k + 1) * WIDTH])
        square = mixed * mixed
        total = jnp.concatenate([run_sum(square[:, o : o + 256], ones32) for o in (0, 256)], axis=1)
        inv = lax.rsqrt(total + NORM_EPS)
        unit = mixed * inv
        getattr(r, name + "inv")[b] = inv
        getattr(r, name + "unit")[b] = unit
        getattr(r, name + "half")[b] = unit.astype(BF16)
    r.vhalf[b] = mm(x, r.qkv_weight_v[b, :, 2 * WIDTH : 3 * WIDTH]).astype(BF16)


def attention(r, b, begin=0, end=WINDOWS):
    tokens = slice(begin * 64, end * 64)
    count = end - begin

    def attend(g):
        cols = group_lanes(g)
        lanes = head_lanes(BF16)
        ones64 = same_run(256, 64)
        q, k, v = r.qhalf[b, tokens, cols], r.khalf[b, tokens, cols], r.vhalf[b, tokens, cols]
        cosine = jnp.concatenate(
            [mm_nt(window(q, w), expand(window(k, w), lanes)) for w in range(count)], axis=0
        )
        r.cosine[b, g, tokens, :] = cosine
        bias = jnp.concatenate([r.bias[b, g]] * count, axis=0)
        expo = jnp.exp(cosine * r.scale[b, g] + bias) * r.mask[b, tokens, :]
        probs = expo / run_sum(expo, ones64)
        r.probs[b, g, tokens, :] = probs
        half = probs.astype(BF16)
        out = [mm(window(half, w), expand(window(v, w), lanes)) for w in range(count)]
        r.attended[b, tokens, cols] = jnp.concatenate(out, axis=0).astype(BF16)

    for g in range(GROUPS):
        attend(g)


def finish_block(r, b, tokens):
    z = mm(r.attended[b, tokens, :], r.proj_weight_v[b])
    centred = z - jnp.mean(z, axis=-1, keepdims=True)
    inverse = lax.rsqrt(jnp.mean(centred * centred, axis=-1, keepdims=True) + LAYER_EPS)
    normed = centred * inverse
    r.inverse[b, tokens, :] = inverse
    r.normed[b, tokens, :] = normed
    if b == 1:
        return None
    return (r.x[b, tokens, :].astype(F32) + normed * r.norm_gain[b : b + 1, :]).astype(BF16)


def backward_norm(r, b, factor):
    grad = r.grad[...].astype(F32)
    normed = r.normed[b]
    gain_term = jnp.sum(grad * normed, axis=0, keepdims=True) * factor
    row = iota((32, 128), 0)
    rest = jnp.zeros((32, 128), F32)
    for k in range(4):
        rest = jnp.where(row == k, gain_term[:, k * 128 : k * 128 + 128], rest)
    r.small[b, 256:288, :] = rest.astype(BF16)
    scaled = grad * r.norm_gain[b : b + 1, :]
    first = jnp.mean(scaled, axis=-1, keepdims=True)
    second = jnp.mean(scaled * normed, axis=-1, keepdims=True)
    dz = (r.inverse[b] * (scaled - first - normed * second)).astype(BF16)
    r.dz[...] = dz
    r.datt[...] = mm_nt(dz, r.proj_weight_v[b]).astype(BF16)


def backward_values(r, b):
    wide = head_lanes(F32)
    for g in range(GROUPS):
        cols = group_lanes(g)
        half, datt = r.probs[b, g].astype(BF16), r.datt[:, cols]
        dv = [collapse(mm_tn(window(half, w), window(datt, w)), wide) for w in range(WINDOWS)]
        r.dmixed[:, group_lanes(g, 2 * WIDTH)] = jnp.concatenate(dv, axis=0).astype(BF16)


def backward_scores(r, b):
    lanes = head_lanes(BF16)
    ones64 = same_run(256, 64)
    for g in range(GROUPS):
        cols = group_lanes(g)
        v, datt, probs = r.vhalf[b, :, cols], r.datt[:, cols], r.probs[b, g]
        dprobs = jnp.concatenate(
            [mm_nt(window(datt, w), expand(window(v, w), lanes)) for w in range(WINDOWS)], axis=0
        )
        dscores = probs * (dprobs - run_sum(probs * dprobs, ones64))
        r.dtab[g] = sum(window(dscores, w) for w in range(WINDOWS))
        r.dlog[g] = jnp.sum(dscores * r.cosine[b, g], axis=0, keepdims=True)
        r.dcos[g] = (dscores * r.scale[b, g]).astype(BF16)


def backward_keys(r, b, begin, end, first, last):
    tokens = slice(first * 64, last * 64)
    lanes, wide = head_lanes(BF16), head_lanes(F32)
    ones32 = same_run(128, 32)
    for g in range(begin, end):
        cols = group_lanes(g)
        q, k, dcos = r.qhalf[b, tokens, cols], r.khalf[b, tokens, cols], r.dcos[g, tokens, :]
        dq, dk = [], []
        for w in range(last - first):
            dq.append(mm(window(dcos, w), expand(window(k, w), lanes)))
            dk.append(collapse(mm_tn(window(dcos, w), window(q, w)), wide))
        for base, parts, unit, inv in ((0, dq, r.qunit, r.qinv), (WIDTH, dk, r.kunit, r.kinv)):
            grad = jnp.concatenate(parts, axis=0)
            unit = unit[b, tokens, cols]
            grad = (grad - unit * rough_sum(unit * grad, ones32)) * inv[b, tokens, cols]
            r.dmixed[tokens, group_lanes(g, base)] = grad.astype(BF16)


def backward_tokens(r, b, tokens=slice(0, TOKENS)):
    grad = r.grad[tokens, :].astype(F32) + mm_nt(r.dmixed[tokens, :], r.qkv_weight_v[b])
    return grad.astype(BF16)


def small_part(r, b, factor):
    ones64 = same_run(256, 64)
    row = iota((32, 128), 0)
    rest = r.small[b, 256:288, :].astype(F32)
    for g in range(GROUPS):
        term = (r.dtab[g] * r.slope[b, g] * factor).astype(BF16)
        total = run_sum(jnp.concatenate([r.dlog[g]] * 8, axis=0), ones64) * (r.scale[b, g] * factor)
        for k in range(2):
            at = table_row(2 * g + k)
            r.small[b, at : at + 64, :] = term[:, k * 128 : k * 128 + 128]
            rest = jnp.where(row == 8 + 2 * g + k, total[0:1, k * 128 : k * 128 + 128], rest)
    r.small[b, 256:288, :] = rest.astype(BF16)
    r.small[b, 544:576, :] = jnp.zeros((32, 128), BF16)


def turn(r, b, g):
    left = r.attended if g == 3 else r.x
    r.turned[b, g] = mm_nt(r.row_order_v[ORDER_OF[b][g]], left[b]).astype(BF16)


def weight_part(r, b, g, factor):
    right = r.dz[...] if g == 3 else r.dmixed[:, g * WIDTH : (g + 1) * WIDTH]
    r.part[b, g] = (mm(r.turned[b, g], right) * factor).astype(BF16)


INPUTS = (
    "fields", "cotangent", "surface", "qkv_weight", "proj_weight", "norm_gain", "log_scale", "pos_table",
    "token_order", "row_order",
)
OUTPUTS = ("d_fields", "d_qkv", "d_proj", "total")


def pick(order, block):
    return mm(order, block).astype(BF16)


def kernel(factor, *refs):
    r = Refs()
    for name, ref in zip(INPUTS + OUTPUTS + tuple(scratch_spec()), refs):
        setattr(r, name, ref)
    links = Links(r)
    loads = Loads(r)
    to_window, window_to_part, to_part, to_shifted, from_window, part_to_window, from_shifted = range(7)
    order = r.token_order_v
    loads.start("fields")
    loads.start("token_order")
    loads.start("qkv_weight", 0)
    loads.start("pos_table", 0)
    loads.start("cotangent")
    loads.start("proj_weight", 0)
    loads.start("row_order")
    loads.start("qkv_weight", 1)
    loads.start("pos_table", 1)
    loads.start("proj_weight", 1)
    links.meet()
    second = [Reduce(r, links, 1, g) for g in range(PARTS)]
    first = [Reduce(r, links, 0, g) for g in range(PARTS)]
    small_second, small_first = SmallSum(r, links, 1), SmallSum(r, links, 0)

    masks(r, links, 0)
    loads.wait("fields")
    loads.wait("token_order")
    r.x[0] = pick(order[to_window], r.fields_v[...])
    loads.wait("qkv_weight", 0)
    project(r, 0)
    loads.wait("pos_table", 0)
    tables(r, 0)
    loads.wait("proj_weight", 0)
    hid = []
    attention(r, 0)
    for k in range(2):
        tokens = slice(k * 128, k * 128 + 128)
        hidden = finish_block(r, 0, tokens)
        for at, count in SPANS[k]:
            r.hid_out[at : at + count, :] = pick(order[window_to_part, at : at + count, tokens], hidden)
        if k == 0:
            links.met()
        hid += links.halo(r.hid_out, r.hid_in, -1, SPANS[k])
    loads.wait("cotangent")
    r.cot_out[...] = pick(order[to_part], r.cotangent_v[...])
    cot = links.halo(r.cot_out, r.cot_in, -1, SPANS[0] + SPANS[1])
    masks(r, links, 1)
    loads.wait("pos_table", 1)
    tables(r, 1)
    loads.wait("row_order")
    for g in range(PARTS):
        turn(r, 0, g)
    loads.wait("qkv_weight", 1)
    loads.wait("proj_weight", 1)
    for copy in hid:
        copy.wait_recv()
    r.x[1] = pick(order[to_shifted], r.hid_in[...])
    project(r, 1)
    attention(r, 1)
    finish_block(r, 1, slice(0, TOKENS))
    for copy in cot:
        copy.wait_recv()
    r.grad[...] = pick(order[to_shifted], r.cot_in[...])
    backward_norm(r, 1, factor)
    backward_values(r, 1)
    backward_scores(r, 1)
    small_part(r, 1, factor)
    small_second.advance()
    back = []
    backward_keys(r, 1, 0, GROUPS, 0, WINDOWS)
    for k in range(2):
        tokens = slice(k * 128, k * 128 + 128)
        grad = backward_tokens(r, 1, tokens)
        for at, count in SHIFTED_SPANS[k]:
            r.back_out[at : at + count, :] = pick(order[from_shifted, at : at + count, tokens], grad)
        back += links.halo(r.back_out, r.back_in, 1, SHIFTED_SPANS[k])

    small_second.advance()
    for g in (3, 2, 1, 0):
        turn(r, 1, g)
        weight_part(r, 1, g, factor)
        second[g].advance()
    for g in (3, 2, 1):
        second[g].advance()
    for copy in back:
        copy.wait_recv()
    second[0].advance()
    r.grad[...] = pick(order[part_to_window], r.back_in[...])
    backward_norm(r, 0, factor)
    small_second.advance()
    weight_part(r, 0, 3, factor)
    first[3].advance()
    backward_values(r, 0)
    weight_part(r, 0, 2, factor)
    first[2].advance()
    first[3].advance()
    backward_scores(r, 0)
    small_part(r, 0, factor)
    small_first.advance()
    first[2].advance()
    backward_keys(r, 0, 0, 2, 0, WINDOWS)
    small_first.advance()
    backward_keys(r, 0, 2, 4, 0, WINDOWS)
    weight_part(r, 0, 0, factor)
    first[0].advance()
    weight_part(r, 0, 1, factor)
    first[1].advance()
    first[0].advance()
    first[1].advance()
    small_second.advance()
    r.d_fields[...] = pick(order[from_window], backward_tokens(r, 0))
    small_first.advance()
    first[3].advance()
    first[2].advance()
    for job in second:
        job.advance()
    small_second.advance()
    small_first.advance()
    first[0].advance()
    first[1].advance()
    links.finish()
    small_second.advance()
    for job in second:
        job.advance()
    first[3].advance()
    small_first.advance()
    first[0].advance()
    first[1].advance()
    first[2].advance()
    small_first.advance()
    links.finish()


def deliver(fields, qkv, proj, total, d_fields, d_qkv, d_proj, d_gain, d_log, d_table):
    d_fields[...] = fields[...]
    d_qkv[...] = qkv[...]
    d_proj[...] = proj[...]
    lane = iota((1, 16), 1)
    for b in range(2):
        for k in range(8):
            at = table_row(k)
            piece = total[b, at : at + 64, :].astype(F32)
            d_table[b, 2 * k] = piece[:, 0:64]
            d_table[b, 2 * k + 1] = piece[:, 64:128]
        rest = total[b, 256:272, :].astype(F32)
        for k in range(4):
            d_gain[b : b + 1, k * 128 : k * 128 + 128] = rest[k : k + 1, :]
        row = jnp.zeros((1, 16), F32)
        for h in range(16):
            spot = rest[8 + h // 2 : 9 + h // 2, h % 2 * 64 : h % 2 * 64 + 1]
            row = jnp.where(lane == h, spot, row)
        d_log[b : b + 1, :] = row


def local(fields, cotangent, surface, qkv_weight, proj_weight, norm_gain, log_scale, pos_table):
    factor = 1.0 / math.sqrt(TOKENS * 128)
    shape = jax.ShapeDtypeStruct
    orders = [jnp.asarray(x, BF16) for x in (token_orders(), row_orders())]
    vmem = pl.BlockSpec(memory_space=pltpu.VMEM)
    any_space = pl.BlockSpec(memory_space=pl.ANY)
    smem = pl.BlockSpec(memory_space=pltpu.SMEM)

    def body(*refs):
        kernel(factor, *refs)

    out = pl.pallas_call(
        body,
        out_shape=[
            shape((TOKENS, WIDTH), BF16),
            shape((2, 4, 3 * WIDTH), F32),
            shape((2, 4, WIDTH), F32),
            shape((2, 2 * HALFROWS, 128), BF16),
        ],
        in_specs=[any_space] * 2 + [vmem] + [any_space] * 2 + [vmem, smem] + [any_space] * 3,
        out_specs=[vmem] * 4,
        scratch_shapes=list(scratch_spec().values()),
        compiler_params=pltpu.CompilerParams(
            collective_id=0, has_side_effects=True, vmem_limit_bytes=60 * 1024 * 1024
        ),
    )(
        fields.reshape(TOKENS, WIDTH), cotangent.reshape(TOKENS, WIDTH), surface, qkv_weight, proj_weight,
        norm_gain, log_scale, pos_table, *orders,
    )
    out = pl.pallas_call(
        deliver,
        out_shape=[
            shape((TOKENS, WIDTH), BF16),
            shape((2, 4, 3 * WIDTH), F32),
            shape((2, 4, WIDTH), F32),
            shape((2, WIDTH), F32),
            shape((2, 16), F32),
            shape((2, 16, 64, 64), F32),
        ],
        in_specs=[vmem] * 4,
        out_specs=[vmem] * 6,
    )(*out)
    return (out[0].reshape(LON, LAT, WIDTH),) + tuple(out[1:])


def solution(mesh):
    placed = (P("lon", "lat", None), P("lon", "lat", None), P(), P(), P(), P(), P(), P())
    return jax.shard_map(
        local,
        mesh=mesh,
        in_specs=placed,
        out_specs=(
            P("lon", "lat", None),
            P(None, ("lon", "lat"), None),
            P(None, ("lon", "lat"), None),
            P(),
            P(),
            P(),
        ),
        check_vma=False,
    )
```

```python
import math

import jax
import jax.numpy as jnp
import numpy as np
from jax import lax
from jax.experimental import pallas as pl
from jax.experimental.pallas import tpu as pltpu
from jax.sharding import PartitionSpec as P

WIN = 8
HALF = WIN // 2
LON, LAT = 8, 32
TOKENS = LON * LAT
WINDOWS = 4
WIDTH = 512
GROUPS = 4
PARTS = 4
HALFROWS = 288
PIECE = 96
NORM_EPS = 1e-06
LAYER_EPS = 1e-05
CAP = 16.0
F32, BF16 = jnp.float32, jnp.bfloat16
MESH = pl.DeviceIdType.MESH

FAR_FIRST = (10, 6, 14, 9, 11, 2, 8, 5, 7, 13, 15, 1, 3, 4, 12)

SPANS = (((0, 48), (112, 48), (224, 16), (240, 16)), ((48, 64), (160, 64)))
SHIFTED_SPANS = (((0, 64), (112, 64)), ((64, 48), (176, 48), (224, 16), (240, 16)))

ORDERS = (("x", "y", "z"), ("y", "z", "x"), ("z", "x", "y"))
ORDER_OF = ((0, 1, 2, 0), (0, 1, 2, 1))


def token_orders():
    cells = [(i, l) for i in range(LON) for l in range(LAT)]
    natural = {c: k for k, c in enumerate(cells)}
    windows = [(i, w * WIN + j) for w in range(WINDOWS) for i in range(WIN) for j in range(WIN)]
    spot = {c: k for k, c in enumerate(windows)}
    parts = []
    for north in (False, True):
        for west in (False, True):
            part = [c for c in cells if (c[0] < HALF) == west and (c[1] < HALF) == north]
            parts += sorted(part, key=lambda c: ((c[1] >= 16) + (c[1] >= 20), c))
    to_window = np.zeros((TOKENS, TOKENS), np.float32)
    to_part = np.zeros_like(to_window)
    window_to_part = np.zeros_like(to_window)
    to_shifted = np.zeros_like(to_window)
    for k, c in enumerate(windows):
        to_window[k, natural[c]] = 1
    for k, c in enumerate(parts):
        to_part[k, natural[c]] = 1
        window_to_part[k, spot[c]] = 1
        to_shifted[spot[((c[0] - HALF) % LON, (c[1] - HALF) % LAT)], k] = 1
    picks = [to_window, window_to_part, to_part, to_shifted]
    picks += [to_window.T, window_to_part.T, to_shifted.T]
    return np.stack(picks)


def row_orders():
    orders = np.zeros((3, WIDTH, WIDTH), np.float32)
    for g, axes in enumerate(ORDERS):
        for place in range(WIDTH):
            at = dict(core=place // 256)
            for axis, step in zip(axes, (64, 16, 4)):
                at[axis] = place // step % 4
            lon = at["z"] % 2 * 16 + at["y"] * 4 + at["x"]
            lat = at["z"] // 2 * 2 + at["core"]
            orders[g, place, (lon * 4 + lat) * 4 + place % 4] = 1
    return orders


def mm(a, b):
    return jnp.dot(a, b, preferred_element_type=F32)


def mm_nt(a, b):
    return lax.dot_general(a, b, (((1,), (1,)), ((), ())), preferred_element_type=F32)


def mm_tn(a, b):
    return lax.dot_general(a, b, (((0,), (0,)), ((), ())), preferred_element_type=F32)


def iota(shape, dim):
    return lax.broadcasted_iota(jnp.int32, shape, dim)


def same_run(size, run):
    return (iota((size, size), 0) // run == iota((size, size), 1) // run).astype(F32).astype(BF16)


def run_sum(x, ones):
    high = x.astype(BF16)
    low = (x - high.astype(F32)).astype(BF16)
    return mm(high, ones) + mm(low, ones)


def rough_sum(x, ones):
    return mm(x.astype(BF16), ones)


def scratch_spec():
    v = pltpu.VMEM
    return dict(
        x=v((2, TOKENS, WIDTH), BF16),
        grad=v((TOKENS, WIDTH), BF16),
        qunit=v((2, TOKENS, WIDTH), F32),
        kunit=v((2, TOKENS, WIDTH), F32),
        qinv=v((2, TOKENS, WIDTH), F32),
        kinv=v((2, TOKENS, WIDTH), F32),
        qhalf=v((2, TOKENS, WIDTH), BF16),
        khalf=v((2, TOKENS, WIDTH), BF16),
        vhalf=v((2, TOKENS, WIDTH), BF16),
        cosine=v((2, GROUPS, TOKENS, 256), F32),
        probs=v((2, GROUPS, TOKENS, 256), F32),
        attended=v((2, TOKENS, WIDTH), BF16),
        normed=v((2, TOKENS, WIDTH), F32),
        inverse=v((2, TOKENS, 1), F32),
        dz=v((TOKENS, WIDTH), BF16),
        datt=v((TOKENS, WIDTH), BF16),
        dmixed=v((TOKENS, 3 * WIDTH), BF16),
        bias=v((2, GROUPS, 64, 256), F32),
        slope=v((2, GROUPS, 64, 256), F32),
        scale=v((2, GROUPS, 1, 256), F32),
        mask=v((2, TOKENS, 256), F32),
        dcos=v((GROUPS, TOKENS, 256), BF16),
        dtab=v((GROUPS, 64, 256), F32),
        dlog=v((GROUPS, 1, 256), F32),
        hid_out=v((TOKENS, WIDTH), BF16),
        hid_in=v((TOKENS, WIDTH), BF16),
        cot_out=v((TOKENS, WIDTH), BF16),
        cot_in=v((TOKENS, WIDTH), BF16),
        back_out=v((TOKENS, WIDTH), BF16),
        back_in=v((TOKENS, WIDTH), BF16),
        turned=v((2, PARTS, WIDTH, TOKENS), BF16),
        part=v((2, PARTS, WIDTH, WIDTH), BF16),
        r1=v((2, PARTS, 256, WIDTH), BF16),
        s1=v((2, PARTS, 256, WIDTH), BF16),
        r2=v((2, PARTS, 3, 64, WIDTH), BF16),
        s2=v((2, PARTS, 16, 16, 128), BF16),
        r3=v((2, PARTS, 16, 16, 128), BF16),
        small=v((2, 2 * HALFROWS, 128), BF16),
        small_r1=v((2, HALFROWS, 128), BF16),
        small_x=v((2, 3, 3, 4, PIECE, 128), BF16),
        send=pltpu.SemaphoreType.DMA((224,)),
        recv=pltpu.SemaphoreType.DMA((224,)),
        load=pltpu.SemaphoreType.DMA((24,)),
        fields_v=v((TOKENS, WIDTH), BF16),
        cotangent_v=v((TOKENS, WIDTH), BF16),
        qkv_weight_v=v((2, WIDTH, 3 * WIDTH), BF16),
        proj_weight_v=v((2, WIDTH, WIDTH), BF16),
        pos_table_v=v((2, 16, 64, 64), F32),
        token_order_v=v((7, TOKENS, TOKENS), BF16),
        row_order_v=v((3, WIDTH, WIDTH), BF16),
    )


class Refs:
    pass


class Links:
    def __init__(self, r):
        self.r = r
        self.count = 0
        self.started = []
        lon, lat = lax.axis_index("lon"), lax.axis_index("lat")
        self.lon, self.lat = lon, lat
        self.core = lat % 2
        self.at = dict(x=lon % 4, y=lon // 4 % 4, z=lat // 2 * 2 + lon // 16)

    def along(self, axis, to, second=None, other=None):
        at = dict(self.at)
        at[axis] = to
        if second is not None:
            at[second] = other
        return (at["z"] % 2 * 16 + at["y"] * 4 + at["x"], at["z"] // 2 * 2 + self.core)

    def sibling(self):
        return (self.lon, self.lat // 2 * 2 + 1 - self.core)

    def shifted(self, dlon, dlat):
        return ((self.lon + dlon + 32) % 32, (self.lat + dlat + 4) % 4)

    def meet(self):
        barrier = pltpu.get_barrier_semaphore()
        others = [self.sibling()]
        for axis in ("x", "y", "z"):
            others += [self.along(axis, (self.at[axis] + d) % 4) for d in (1, 2, 3)]
        for a, b in (("x", "y"), ("y", "z"), ("z", "x")):
            others += [
                self.along(a, (self.at[a] + i) % 4, b, (self.at[b] + j) % 4) for i in (1, 2, 3) for j in (1, 2, 3)
            ]
        for d in (-1, 1):
            others += [self.shifted(d, 0), self.shifted(0, d), self.shifted(d, d)]
        for other in others:
            pl.semaphore_signal(barrier, inc=1, device_id=other, device_id_type=MESH)
        self.others = len(others)

    def met(self):
        pl.semaphore_wait(pltpu.get_barrier_semaphore(), self.others)

    def send(self, src, dst, to):
        k = self.count
        self.count += 1
        copy = pltpu.make_async_remote_copy(
            src_ref=src, dst_ref=dst, send_sem=self.r.send.at[k], recv_sem=self.r.recv.at[k],
            device_id=to, device_id_type=MESH,
        )
        copy.start()
        self.started.append(copy)
        return copy

    def finish(self):
        for copy in self.started:
            copy.wait_send()
        self.started = []

    def halo(self, src, dst, sign, spans):
        copies = []
        for first, count in spans:
            if first < 112:
                dst[first : first + count, :] = src[first : first + count, :]
                continue
            to = (sign, 0) if first < 224 else ((0, sign) if first < 240 else (sign, sign))
            copies.append(self.send(src.at[pl.ds(first, count)], dst.at[pl.ds(first, count)], self.shifted(*to)))
        return copies


class Loads:
    def __init__(self, r):
        self.r = r
        self.copies = {}

    def start(self, name, at=None):
        src, dst = getattr(self.r, name), getattr(self.r, name + "_v")
        if at is not None:
            src, dst = src.at[at], dst.at[at]
        copy = pltpu.make_async_copy(src, dst, self.r.load.at[len(self.copies)])
        copy.start()
        self.copies[name, at] = copy

    def wait(self, name, at=None):
        self.copies[name, at].wait()


def rows(at, size):
    return pl.ds(pl.multiple_of(at * size, size), size)


class Reduce:
    def __init__(self, r, links, b, g):
        self.r, self.links, self.b, self.g = r, links, b, g
        self.axes = ORDERS[ORDER_OF[b][g]]
        self.place = [links.at[a] for a in self.axes]
        self.step = 0

    def peers(self, level):
        axis, place = self.axes[level], self.place[level]
        return [((place + d) % 4, d) for d in (2, 1, 3)]

    def advance(self):
        r, links, b, g = self.r, self.links, self.b, self.g
        step = self.step
        self.step += 1
        if step == 0:
            src = r.part.at[b, g, rows(1 - links.core, 256)]
            self.waits = [links.send(src, r.r1.at[b, g], links.sibling())]
            return
        for copy in self.waits:
            copy.wait_recv()
        if step == 1:
            own = r.part[b, g, rows(links.core, 256), :].astype(F32)
            r.s1[b, g] = (own + r.r1[b, g].astype(F32)).astype(BF16)
            self.waits = [
                links.send(r.s1.at[b, g, rows(k, 64)], r.r2.at[b, g, d - 1], links.along(self.axes[0], k))
                for k, d in self.peers(0)
            ]
        elif step == 2:
            total = r.s1[b, g, rows(self.place[0], 64), :].astype(F32)
            for d in range(3):
                total += r.r2[b, g, d].astype(F32)
            for chip in range(16):
                piece = total[4 * chip : 4 * chip + 4, :]
                piece = jnp.concatenate([piece[:, j * 128 : j * 128 + 128] for j in range(4)], axis=0)
                r.s2[b, g, chip] = piece.astype(BF16)
            (_, one, two), (_, i, j) = self.axes, self.place
            here = i * 4 + j
            r.r3[b, g, here] = r.s2[b, g, here]
            self.waits = []
            for d in FAR_FIRST:
                k, m = (i + d // 4) % 4, (j + d % 4) % 4
                self.waits.append(
                    links.send(r.s2.at[b, g, k * 4 + m], r.r3.at[b, g, here], links.along(one, k, two, m))
                )
        elif step == 3:
            total = r.r3[b, g, 0].astype(F32)
            for k in range(1, 16):
                total += r.r3[b, g, k].astype(F32)
            own = jnp.concatenate([total[4 * j : 4 * j + 4, :] for j in range(4)], axis=1)
            if g == 3:
                r.d_proj[b] = own
            else:
                r.d_qkv[b, :, g * WIDTH : (g + 1) * WIDTH] = own


class SmallSum:
    def __init__(self, r, links, b):
        self.r, self.links, self.b = r, links, b
        self.step = 0

    def exchange(self, level, piece):
        r, links, b = self.r, self.links, self.b
        axis = ORDERS[piece][level]
        place = links.at[axis]
        mine = r.small_x.at[b, level, piece, place]
        return [links.send(mine, mine, links.along(axis, (place + d) % 4)) for d in (2, 1, 3)]

    def advance(self):
        r, links, b = self.r, self.links, self.b
        step = self.step
        self.step += 1
        half = rows(links.core, HALFROWS)
        if step == 0:
            src = r.small.at[b, rows(1 - links.core, HALFROWS)]
            self.waits = [links.send(src, r.small_r1.at[b], links.sibling())]
            return
        for copy in self.waits:
            copy.wait_recv()
        if step == 5:
            return
        self.waits = []
        for piece in range(3):
            span = slice(piece * PIECE, (piece + 1) * PIECE)
            if step == 1:
                first = r.small[b, rows(links.core * 3 + piece, PIECE), :].astype(F32)
                total = first + r.small_r1[b, span, :].astype(F32)
            else:
                total = r.small_x[b, step - 2, piece, 0].astype(F32)
                for k in range(1, 4):
                    total += r.small_x[b, step - 2, piece, k].astype(F32)
            total = total.astype(BF16)
            if step < 4:
                r.small_x[b, step - 1, piece, links.at[ORDERS[piece][step - 1]]] = total
                self.waits += self.exchange(step - 1, piece)
            else:
                r.total[b, rows(links.core * 3 + piece, PIECE), :] = total
        if step == 4:
            mine = r.total.at[b, half]
            self.waits = [links.send(mine, mine, links.sibling())]


def table_row(k):
    return k * 64 + (HALFROWS - 256) * (k // 4)


def tables(r, b):
    lane = iota((1, 256), 1) // 64
    for g in range(GROUPS):
        logs = jnp.full((1, 256), 0.0, F32) + r.log_scale[b, 4 * g]
        for h in range(1, 4):
            logs = jnp.where(lane == h, r.log_scale[b, 4 * g + h], logs)
        scale = jnp.exp(logs)
        sigma = jnp.concatenate([r.pos_table_v[b, 4 * g + h] for h in range(4)], axis=1)
        sigma = 1.0 / (1.0 + jnp.exp(-sigma))
        r.scale[b, g] = scale
        r.bias[b, g] = CAP * sigma - scale - CAP
        r.slope[b, g] = CAP * sigma * (1.0 - sigma)


def masks(r, links, b):
    shift = HALF * b
    first = r.surface[pl.ds(pl.multiple_of(links.lon * LON, LON), LON), :]
    later = r.surface[pl.ds(pl.multiple_of((links.lon + 1) % 32 * LON, LON), LON), :]
    slab = jnp.concatenate([first, later], axis=0).astype(F32).astype(BF16)

    def column(w, t):
        return (links.lat * LAT + w * WIN + t % WIN + shift) % 128

    def labels(found, col):
        return found * 2.0 + (col < shift).astype(F32)

    for w in range(WINDOWS):
        tok = iota((128, 256), 1) % 64
        pick = (iota((128, 256), 0) == column(w, tok)).astype(F32).astype(BF16)
        wide = mm(slab, pick)
        tok = iota((16, 256), 1) % 64
        found = jnp.sum(jnp.where(iota((16, 256), 0) == tok // WIN + shift, wide, 0.0), axis=0, keepdims=True)
        along = labels(found, column(w, iota((1, 256), 1) % 64))
        tok = iota((64, 128), 0)
        pick = (iota((64, 128), 1) == column(w, tok)).astype(F32).astype(BF16)
        tall = mm_nt(pick, slab)
        tok = iota((64, 16), 0)
        found = jnp.sum(jnp.where(iota((64, 16), 1) == tok // WIN + shift, tall, 0.0), axis=1, keepdims=True)
        down = labels(found, column(w, iota((64, 1), 0)))
        r.mask[b, w * 64 : w * 64 + 64, :] = (down == along).astype(F32)


def group_lanes(g, base=0):
    return pl.ds(pl.multiple_of(base + g * 128, 128), 128)


def head_lanes(dtype):
    lane = iota((1, 128), 1) // 32
    return [(lane == h).astype(F32).astype(dtype) for h in range(4)]


def expand(block, lanes):
    return jnp.concatenate([block * lanes[h] for h in range(4)], axis=0)


def collapse(block, lanes):
    return sum(block[h * 64 : h * 64 + 64, :] * lanes[h] for h in range(4))


def window(x, w):
    return x[w * 64 : w * 64 + 64, :]


def project(r, b):
    x = r.x[b]
    ones32 = same_run(256, 32)
    for name, k in (("q", 0), ("k", 1)):
        mixed = mm(x, r.qkv_weight_v[b, :, k * WIDTH : (k + 1) * WIDTH])
        square = mixed * mixed
        total = jnp.concatenate([run_sum(square[:, o : o + 256], ones32) for o in (0, 256)], axis=1)
        inv = lax.rsqrt(total + NORM_EPS)
        unit = mixed * inv
        getattr(r, name + "inv")[b] = inv
        getattr(r, name + "unit")[b] = unit
        getattr(r, name + "half")[b] = unit.astype(BF16)
    r.vhalf[b] = mm(x, r.qkv_weight_v[b, :, 2 * WIDTH : 3 * WIDTH]).astype(BF16)


def attention(r, b, begin=0, end=WINDOWS):
    tokens = slice(begin * 64, end * 64)
    count = end - begin

    def attend(g):
        cols = group_lanes(g)
        lanes = head_lanes(BF16)
        ones64 = same_run(256, 64)
        q, k, v = r.qhalf[b, tokens, cols], r.khalf[b, tokens, cols], r.vhalf[b, tokens, cols]
        cosine = jnp.concatenate(
            [mm_nt(window(q, w), expand(window(k, w), lanes)) for w in range(count)], axis=0
        )
        r.cosine[b, g, tokens, :] = cosine
        bias = jnp.concatenate([r.bias[b, g]] * count, axis=0)
        expo = jnp.exp(cosine * r.scale[b, g] + bias) * r.mask[b, tokens, :]
        probs = expo / run_sum(expo, ones64)
        r.probs[b, g, tokens, :] = probs
        half = probs.astype(BF16)
        out = [mm(window(half, w), expand(window(v, w), lanes)) for w in range(count)]
        r.attended[b, tokens, cols] = jnp.concatenate(out, axis=0).astype(BF16)

    for g in range(GROUPS):
        attend(g)


def finish_block(r, b, tokens):
    z = mm(r.attended[b, tokens, :], r.proj_weight_v[b])
    centred = z - jnp.mean(z, axis=-1, keepdims=True)
    inverse = lax.rsqrt(jnp.mean(centred * centred, axis=-1, keepdims=True) + LAYER_EPS)
    normed = centred * inverse
    r.inverse[b, tokens, :] = inverse
    r.normed[b, tokens, :] = normed
    if b == 1:
        return None
    return (r.x[b, tokens, :].astype(F32) + normed * r.norm_gain[b : b + 1, :]).astype(BF16)


def backward_norm(r, b, factor):
    grad = r.grad[...].astype(F32)
    normed = r.normed[b]
    gain_term = jnp.sum(grad * normed, axis=0, keepdims=True) * factor
    row = iota((32, 128), 0)
    rest = jnp.zeros((32, 128), F32)
    for k in range(4):
        rest = jnp.where(row == k, gain_term[:, k * 128 : k * 128 + 128], rest)
    r.small[b, 256:288, :] = rest.astype(BF16)
    scaled = grad * r.norm_gain[b : b + 1, :]
    first = jnp.mean(scaled, axis=-1, keepdims=True)
    second = jnp.mean(scaled * normed, axis=-1, keepdims=True)
    dz = (r.inverse[b] * (scaled - first - normed * second)).astype(BF16)
    r.dz[...] = dz
    r.datt[...] = mm_nt(dz, r.proj_weight_v[b]).astype(BF16)


def backward_values(r, b):
    wide = head_lanes(F32)
    for g in range(GROUPS):
        cols = group_lanes(g)
        half, datt = r.probs[b, g].astype(BF16), r.datt[:, cols]
        dv = [collapse(mm_tn(window(half, w), window(datt, w)), wide) for w in range(WINDOWS)]
        r.dmixed[:, group_lanes(g, 2 * WIDTH)] = jnp.concatenate(dv, axis=0).astype(BF16)


def backward_scores(r, b):
    lanes = head_lanes(BF16)
    ones64 = same_run(256, 64)
    for g in range(GROUPS):
        cols = group_lanes(g)
        v, datt, probs = r.vhalf[b, :, cols], r.datt[:, cols], r.probs[b, g]
        dprobs = jnp.concatenate(
            [mm_nt(window(datt, w), expand(window(v, w), lanes)) for w in range(WINDOWS)], axis=0
        )
        dscores = probs * (dprobs - run_sum(probs * dprobs, ones64))
        r.dtab[g] = sum(window(dscores, w) for w in range(WINDOWS))
        r.dlog[g] = jnp.sum(dscores * r.cosine[b, g], axis=0, keepdims=True)
        r.dcos[g] = (dscores * r.scale[b, g]).astype(BF16)


def backward_keys(r, b, begin, end, first, last):
    tokens = slice(first * 64, last * 64)
    lanes, wide = head_lanes(BF16), head_lanes(F32)
    ones32 = same_run(128, 32)
    for g in range(begin, end):
        cols = group_lanes(g)
        q, k, dcos = r.qhalf[b, tokens, cols], r.khalf[b, tokens, cols], r.dcos[g, tokens, :]
        dq, dk = [], []
        for w in range(last - first):
            dq.append(mm(window(dcos, w), expand(window(k, w), lanes)))
            dk.append(collapse(mm_tn(window(dcos, w), window(q, w)), wide))
        for base, parts, unit, inv in ((0, dq, r.qunit, r.qinv), (WIDTH, dk, r.kunit, r.kinv)):
            grad = jnp.concatenate(parts, axis=0)
            unit = unit[b, tokens, cols]
            grad = (grad - unit * rough_sum(unit * grad, ones32)) * inv[b, tokens, cols]
            r.dmixed[tokens, group_lanes(g, base)] = grad.astype(BF16)


def backward_tokens(r, b, tokens=slice(0, TOKENS)):
    grad = r.grad[tokens, :].astype(F32) + mm_nt(r.dmixed[tokens, :], r.qkv_weight_v[b])
    return grad.astype(BF16)


def small_part(r, b, factor):
    ones64 = same_run(256, 64)
    row = iota((32, 128), 0)
    rest = r.small[b, 256:288, :].astype(F32)
    for g in range(GROUPS):
        term = (r.dtab[g] * r.slope[b, g] * factor).astype(BF16)
        total = run_sum(jnp.concatenate([r.dlog[g]] * 8, axis=0), ones64) * (r.scale[b, g] * factor)
        for k in range(2):
            at = table_row(2 * g + k)
            r.small[b, at : at + 64, :] = term[:, k * 128 : k * 128 + 128]
            rest = jnp.where(row == 8 + 2 * g + k, total[0:1, k * 128 : k * 128 + 128], rest)
    r.small[b, 256:288, :] = rest.astype(BF16)
    r.small[b, 544:576, :] = jnp.zeros((32, 128), BF16)


def turn(r, b, g):
    left = r.attended if g == 3 else r.x
    r.turned[b, g] = mm_nt(r.row_order_v[ORDER_OF[b][g]], left[b]).astype(BF16)


def weight_part(r, b, g, factor):
    right = r.dz[...] if g == 3 else r.dmixed[:, g * WIDTH : (g + 1) * WIDTH]
    r.part[b, g] = (mm(r.turned[b, g], right) * factor).astype(BF16)


INPUTS = (
    "fields", "cotangent", "surface", "qkv_weight", "proj_weight", "norm_gain", "log_scale", "pos_table",
    "token_order", "row_order",
)
OUTPUTS = ("d_fields", "d_qkv", "d_proj", "total")


def pick(order, block):
    return mm(order, block).astype(BF16)


def kernel(factor, *refs):
    r = Refs()
    for name, ref in zip(INPUTS + OUTPUTS + tuple(scratch_spec()), refs):
        setattr(r, name, ref)
    links = Links(r)
    loads = Loads(r)
    to_window, window_to_part, to_part, to_shifted, from_window, part_to_window, from_shifted = range(7)
    order = r.token_order_v
    loads.start("fields")
    loads.start("token_order")
    loads.start("qkv_weight", 0)
    loads.start("pos_table", 0)
    loads.start("cotangent")
    loads.start("proj_weight", 0)
    loads.start("row_order")
    loads.start("qkv_weight", 1)
    loads.start("pos_table", 1)
    loads.start("proj_weight", 1)
    links.meet()
    second = [Reduce(r, links, 1, g) for g in range(PARTS)]
    first = [Reduce(r, links, 0, g) for g in range(PARTS)]
    small_second, small_first = SmallSum(r, links, 1), SmallSum(r, links, 0)

    masks(r, links, 0)
    loads.wait("fields")
    loads.wait("token_order")
    r.x[0] = pick(order[to_window], r.fields_v[...])
    loads.wait("qkv_weight", 0)
    project(r, 0)
    loads.wait("pos_table", 0)
    tables(r, 0)
    loads.wait("proj_weight", 0)
    hid = []
    attention(r, 0)
    for k in range(2):
        tokens = slice(k * 128, k * 128 + 128)
        hidden = finish_block(r, 0, tokens)
        for at, count in SPANS[k]:
            r.hid_out[at : at + count, :] = pick(order[window_to_part, at : at + count, tokens], hidden)
        if k == 0:
            links.met()
        hid += links.halo(r.hid_out, r.hid_in, -1, SPANS[k])
    loads.wait("cotangent")
    r.cot_out[...] = pick(order[to_part], r.cotangent_v[...])
    cot = links.halo(r.cot_out, r.cot_in, -1, SPANS[0] + SPANS[1])
    masks(r, links, 1)
    loads.wait("pos_table", 1)
    tables(r, 1)
    loads.wait("row_order")
    for g in range(PARTS):
        turn(r, 0, g)
    loads.wait("qkv_weight", 1)
    loads.wait("proj_weight", 1)
    for copy in hid:
        copy.wait_recv()
    r.x[1] = pick(order[to_shifted], r.hid_in[...])
    project(r, 1)
    attention(r, 1)
    finish_block(r, 1, slice(0, TOKENS))
    for copy in cot:
        copy.wait_recv()
    r.grad[...] = pick(order[to_shifted], r.cot_in[...])
    backward_norm(r, 1, factor)
    backward_values(r, 1)
    backward_scores(r, 1)
    small_part(r, 1, factor)
    small_second.advance()
    back = []
    backward_keys(r, 1, 0, GROUPS, 0, WINDOWS)
    for k in range(2):
        tokens = slice(k * 128, k * 128 + 128)
        grad = backward_tokens(r, 1, tokens)
        for at, count in SHIFTED_SPANS[k]:
            r.back_out[at : at + count, :] = pick(order[from_shifted, at : at + count, tokens], grad)
        back += links.halo(r.back_out, r.back_in, 1, SHIFTED_SPANS[k])

    small_second.advance()
    for g in (3, 2, 1, 0):
        turn(r, 1, g)
        weight_part(r, 1, g, factor)
        second[g].advance()
    for g in (3, 2, 1):
        second[g].advance()
    for copy in back:
        copy.wait_recv()
    second[0].advance()
    r.grad[...] = pick(order[part_to_window], r.back_in[...])
    backward_norm(r, 0, factor)
    small_second.advance()
    weight_part(r, 0, 3, factor)
    first[3].advance()
    backward_values(r, 0)
    weight_part(r, 0, 2, factor)
    first[2].advance()
    first[3].advance()
    backward_scores(r, 0)
    small_part(r, 0, factor)
    small_first.advance()
    first[2].advance()
    backward_keys(r, 0, 0, 2, 0, WINDOWS)
    small_first.advance()
    backward_keys(r, 0, 2, 4, 0, WINDOWS)
    weight_part(r, 0, 0, factor)
    first[0].advance()
    weight_part(r, 0, 1, factor)
    first[1].advance()
    first[0].advance()
    first[1].advance()
    small_second.advance()
    r.d_fields[...] = pick(order[from_window], backward_tokens(r, 0))
    small_first.advance()
    first[3].advance()
    first[2].advance()
    for job in second:
        job.advance()
    small_second.advance()
    small_first.advance()
    first[0].advance()
    first[1].advance()
    links.finish()
    small_second.advance()
    for job in second:
        job.advance()
    first[3].advance()
    small_first.advance()
    first[0].advance()
    first[1].advance()
    first[2].advance()
    small_first.advance()
    links.finish()


def deliver(fields, qkv, proj, total, d_fields, d_qkv, d_proj, d_gain, d_log, d_table):
    d_fields[...] = fields[...]
    d_qkv[...] = qkv[...]
    d_proj[...] = proj[...]
    lane = iota((1, 16), 1)
    for b in range(2):
        for k in range(8):
            at = table_row(k)
            piece = total[b, at : at + 64, :].astype(F32)
            d_table[b, 2 * k] = piece[:, 0:64]
            d_table[b, 2 * k + 1] = piece[:, 64:128]
        rest = total[b, 256:272, :].astype(F32)
        for k in range(4):
            d_gain[b : b + 1, k * 128 : k * 128 + 128] = rest[k : k + 1, :]
        row = jnp.zeros((1, 16), F32)
        for h in range(16):
            spot = rest[8 + h // 2 : 9 + h // 2, h % 2 * 64 : h % 2 * 64 + 1]
            row = jnp.where(lane == h, spot, row)
        d_log[b : b + 1, :] = row


def local(fields, cotangent, surface, qkv_weight, proj_weight, norm_gain, log_scale, pos_table):
    factor = 1.0 / math.sqrt(TOKENS * 128)
    shape = jax.ShapeDtypeStruct
    orders = [jnp.asarray(x, BF16) for x in (token_orders(), row_orders())]
    vmem = pl.BlockSpec(memory_space=pltpu.VMEM)
    any_space = pl.BlockSpec(memory_space=pl.ANY)
    smem = pl.BlockSpec(memory_space=pltpu.SMEM)

    def body(*refs):
        kernel(factor, *refs)

    out = pl.pallas_call(
        body,
        out_shape=[
            shape((TOKENS, WIDTH), BF16),
            shape((2, 4, 3 * WIDTH), F32),
            shape((2, 4, WIDTH), F32),
            shape((2, 2 * HALFROWS, 128), BF16),
        ],
        in_specs=[any_space] * 2 + [vmem] + [any_space] * 2 + [vmem, smem] + [any_space] * 3,
        out_specs=[vmem] * 4,
        scratch_shapes=list(scratch_spec().values()),
        compiler_params=pltpu.CompilerParams(
            collective_id=0, has_side_effects=True, vmem_limit_bytes=60 * 1024 * 1024
        ),
    )(
        fields.reshape(TOKENS, WIDTH), cotangent.reshape(TOKENS, WIDTH), surface, qkv_weight, proj_weight,
        norm_gain, log_scale, pos_table, *orders,
    )
    out = pl.pallas_call(
        deliver,
        out_shape=[
            shape((TOKENS, WIDTH), BF16),
            shape((2, 4, 3 * WIDTH), F32),
            shape((2, 4, WIDTH), F32),
            shape((2, WIDTH), F32),
            shape((2, 16), F32),
            shape((2, 16, 64, 64), F32),
        ],
        in_specs=[vmem] * 4,
        out_specs=[vmem] * 6,
    )(*out)
    return (out[0].reshape(LON, LAT, WIDTH),) + tuple(out[1:])


def solution(mesh):
    placed = (P("lon", "lat", None), P("lon", "lat", None), P(), P(), P(), P(), P(), P())
    return jax.shard_map(
        local,
        mesh=mesh,
        in_specs=placed,
        out_specs=(
            P("lon", "lat", None),
            P(None, ("lon", "lat"), None),
            P(None, ("lon", "lat"), None),
            P(),
            P(),
            P(),
        ),
        check_vma=False,
    )
```
